32 devices in a mesh: group: 2 (over y), query: 4 (over x, core), memory: 4 (over z).
Axes of the slice: x: 2, y: 2, z: 4, core: 2. Of those that a mesh axis runs over, the one named last changes fastest.
Arguments:
- queries: bfloat16 [4096, 2048], P(('group', 'query', 'memory')), parts along dimension 0, may hold values from -140 to 140
- keys: bfloat16 [8192, 2048], P(('group', 'memory'), 'query'), parts along dimension 0, may hold values from -6.1 to 6.1
- values: bfloat16 [8192, 2048], P(('group', 'memory'), 'query'), parts along dimension 0, may hold values from -6 to 6
- grad_out: bfloat16 [4096, 2048], P(('group', 'query', 'memory')), parts along dimension 0, may hold values from -6 to 6
- blocks: int32 [16, 32, 2], P(None, 'group'), parts along dimension 1, may hold values from 0 to 31, as said below
Outputs:
- grad_q: bfloat16 [4096, 2048], P(('group', 'query', 'memory')), parts along dimension 0
- grad_k: bfloat16 [8192, 2048], P(('group', 'memory'), 'query'), parts along dimension 0
- grad_v: bfloat16 [8192, 2048], P(('group', 'memory'), 'query'), parts along dimension 0
The draws below stay inside these ranges and needn't reach their ends.
There are 2 independent parts, one for each index of `group`. The reference program is written for one: setup_inputs(seed, part) draws one part's arguments, and reference() takes and returns one part's arrays. A program takes and returns all parts, laid end to end along the dimension named above; each array names one. Nothing has to cross between parts.
Inputs may be any that keep to these rules, and one draw needn't show every extreme that they name: blocks[h, b, 0] and blocks[h, b, 1] are two different memory blocks of 128 rows.
All inputs are finite; a program needn't handle non-finite values.
Results may differ from the reference program's by a relative error of at most 0.0056.
Values may be sent and summed in bfloat16 or wider, within the bound.
A program may use at most 128 MiB of HBM per device.

```python
import math
import jax
import jax.numpy as jnp
from jax import lax

HEADS = 16
HEAD_DIM = 128
BLOCK = 128
IMAGE_TOK = 1024
NQ = 2048
NM = 4096
NQB = 16
NMB = 32
HD = 2048


def make_blocks(key):
    key = jax.random.fold_in(key, 11)
    key_weight, key_first, key_second, key_offset, key_other = jax.random.split(key, 5)
    pictures = NM // IMAGE_TOK
    per_picture = IMAGE_TOK // BLOCK
    weights = jnp.left_shift(jnp.ones((pictures,), jnp.int32), jax.random.randint(key_weight, (pictures,), 0, 4))
    bounds = jnp.cumsum(weights)
    total = bounds[-1]

    def pick_picture(sub_key):
        ticket = jax.random.randint(sub_key, (HEADS, NQB), 0, total)
        return jnp.sum((ticket[:, :, None] >= bounds[None, None, :]).astype(jnp.int32), axis=-1)
    first_picture = pick_picture(key_first)
    second_picture = pick_picture(key_second)
    first_offset = jax.random.randint(key_offset, (HEADS, NQB), 0, per_picture)
    second_offset = jax.random.randint(key_other, (HEADS, NQB), 0, per_picture)
    first_block = first_picture * per_picture + first_offset
    second_block = second_picture * per_picture + second_offset
    second_block = jnp.where(second_block == first_block, second_picture * per_picture + (second_offset + 1) % per_picture, second_block)
    return jnp.stack([first_block, second_block], axis=-1).astype(jnp.int32)


def base_keys(key):
    key = jax.random.fold_in(key, 7)
    return jnp.clip(jax.random.normal(key, (NM, HEADS * HEAD_DIM), jnp.float32), -6.0, 6.0)


def draw_blocks(key, part):
    return make_blocks(key)


def draw_keys(key, part):
    shared = base_keys(key)
    return shared.astype(jnp.bfloat16)


def draw_queries(key, part):
    key = jax.random.fold_in(key, 5)
    result = jnp.clip(jax.random.normal(key, (NQ, HEADS * HEAD_DIM), jnp.float32), -6.0, 6.0)
    return result.astype(jnp.bfloat16)


def shard_levels(rng, extent, cuts, least, top_value):
    gain, own = 1.0, jax.random.fold_in(rng, 6)
    for axis_at, blocks in cuts:
        steps = jnp.exp(jax.random.uniform(jax.random.fold_in(own, axis_at), (blocks,), jnp.float32, least / len(cuts), top_value / len(cuts)))
        gain = gain * jnp.repeat(steps, extent[axis_at] // blocks).reshape([-1 if axis == axis_at else 1 for axis in range(len(extent))])
    return gain


def scatter_about(key, dims, width, limit, cuts=(), held_as=jnp.bfloat16):
    values = jax.random.normal(key, dims, jnp.float32) * width
    if len(cuts) > 0:
        values = shard_levels(key, dims, cuts, -0.22, 0.18) * values
    return jnp.clip(values, min=-limit, max=limit).astype(held_as)


def setup_inputs(seed: int = 0, part: int = 0) -> dict:
    key_list = jax.random.split(jax.random.key(seed), 6)
    part_keys = jax.random.split(jax.random.fold_in(key_list[5], part), 6)
    return {
        "queries": draw_queries(jax.random.fold_in(jax.random.fold_in(key_list[5], part), 71), part),
        "keys": draw_keys(jax.random.fold_in(jax.random.fold_in(key_list[5], part), 71), part),
        "values": scatter_about(part_keys[2], (NM, HD), 1.0, 6.0, ((0, 4), (1, 4))),
        "grad_out": scatter_about(part_keys[3], (NQ, HD), 1.0, 6.0, ((0, 16),)),
        "blocks": draw_blocks(jax.random.fold_in(jax.random.fold_in(key_list[5], part), 71), part),
    }


def head_backward(inputs):
    query_head, grad_head, key_head, value_head, block_ids = inputs
    scale = 1.0 / math.sqrt(HEAD_DIM)
    query_blocks = NQ // BLOCK
    per_picture = IMAGE_TOK // BLOCK
    query_rows = query_head.reshape(query_blocks, BLOCK, HEAD_DIM).astype(jnp.float32)
    grad_rows = grad_head.reshape(query_blocks, BLOCK, HEAD_DIM).astype(jnp.float32)
    key_blocks = key_head.reshape(NMB, BLOCK, HEAD_DIM)[block_ids].astype(jnp.float32)
    value_blocks = value_head.reshape(NMB, BLOCK, HEAD_DIM)[block_ids].astype(jnp.float32)
    scores = jnp.einsum('nbd,nskd->nbsk', query_rows, key_blocks) * scale
    prod_grad = jnp.einsum('nbd,nskd->nbsk', grad_rows, value_blocks)
    row_top = lax.optimization_barrier(jnp.max(scores, axis=(2, 3), keepdims=True))
    log_total = row_top + jnp.log(lax.optimization_barrier(jnp.sum(jnp.exp(scores - row_top), axis=(2, 3), keepdims=True)))
    probs = jnp.exp(scores - log_total)
    delta_row = lax.optimization_barrier(jnp.sum(probs * prod_grad, axis=(2, 3), keepdims=True))
    probs_half = lax.optimization_barrier(probs.astype(jnp.bfloat16)).astype(jnp.float32)
    score_grad = lax.optimization_barrier((probs * (prod_grad - delta_row)).astype(jnp.bfloat16)).astype(jnp.float32)
    value_terms = jnp.einsum('nbsk,nbd->nskd', probs_half, grad_rows)
    key_terms = jnp.einsum('nbsk,nbd->nskd', score_grad, query_rows) * scale
    grad_value = jnp.zeros((NMB, BLOCK, HEAD_DIM), jnp.float32).at[block_ids].add(value_terms)
    grad_key = jnp.zeros((NMB, BLOCK, HEAD_DIM), jnp.float32).at[block_ids].add(key_terms)
    query_terms = jnp.einsum('nbsk,nskd->nbsd', score_grad, key_blocks) * scale
    picture_ids = block_ids // per_picture
    grad_query = jnp.zeros((query_blocks, BLOCK, HEAD_DIM), jnp.float32)
    for neighbour in range(NM // IMAGE_TOK):
        chosen = (picture_ids == neighbour)[:, None, :, None]
        partial_sum = lax.optimization_barrier(jnp.sum(jnp.where(chosen, query_terms, 0.0), axis=2))
        grad_query = grad_query + lax.optimization_barrier(partial_sum.astype(jnp.bfloat16)).astype(jnp.float32)
    return (grad_query.reshape(NQ, HEAD_DIM), grad_key.reshape(NM, HEAD_DIM), grad_value.reshape(NM, HEAD_DIM))

def by_head(array, row_count):
    return array.reshape(row_count, HEADS, HEAD_DIM).transpose(1, 0, 2)

def merge_heads(array, row_count):
    return array.transpose(1, 0, 2).reshape(row_count, HEADS * HEAD_DIM).astype(jnp.bfloat16)

def reference(queries, keys, values, grad_out, blocks):
    grad_query, grad_key, grad_value = lax.map(head_backward, (by_head(queries, NQ), by_head(grad_out, NQ), by_head(keys, NM), by_head(values, NM), blocks))
    return (merge_heads(grad_query, NQ), merge_heads(grad_key, NM), merge_heads(grad_value, NM))
```

```python
import functools
import math

import jax
import jax.numpy as jnp
from jax import lax
from jax.experimental import pallas as pl
from jax.experimental.pallas import tpu as pltpu
from jax.sharding import PartitionSpec as P

HEAD_DIM = 128
BLOCK = 128


def joined(value, axis, combine):
    everything = jax.tree.map(lambda part: lax.all_gather(part, axis), value)
    leading = jax.tree.map(lambda part: part[0], everything)

    def hop(k, so_far):
        return combine(so_far, jax.tree.map(lambda part: part[k], everything))

    return lax.fori_loop(1, lax.axis_size(axis), hop, leading)


def combine_stats(first, second):
    top_value = jnp.maximum(first[0], second[0])
    first_factor = jnp.exp(first[0] - top_value)
    second_factor = jnp.exp(second[0] - top_value)
    return (
        top_value,
        first[1] * first_factor + second[1] * second_factor,
        first[2] * first_factor + second[2] * second_factor,
    )


def local_grads(query_rows, grad_rows, key_rows, value_rows, head_blocks, shard_index):
    row_count = query_rows.shape[0]
    query_blocks = row_count // BLOCK
    local_heads = query_rows.shape[1] // HEAD_DIM
    memory_blocks = key_rows.shape[0] // BLOCK
    slot_count = head_blocks.shape[2]
    group_size = math.gcd(query_blocks, 8)
    group_count = query_blocks // group_size
    scale = 1.0 / math.sqrt(HEAD_DIM)

    def split_queries(array):
        return array.reshape(group_count, group_size, BLOCK, local_heads, HEAD_DIM).transpose(
            3, 0, 1, 2, 4
        )

    def split_memory(array):
        return array.reshape(memory_blocks, BLOCK, local_heads, HEAD_DIM).transpose(2, 0, 1, 3)

    query_split = split_queries(query_rows)
    grad_split = split_queries(grad_rows)
    key_split = split_memory(key_rows)
    value_split = split_memory(value_rows)
    local_ids = head_blocks - shard_index * memory_blocks
    live_slots = ((local_ids >= 0) & (local_ids < memory_blocks)).reshape(
        local_heads, group_count, group_size, slot_count
    )
    slot_picks = jnp.clip(local_ids, 0, memory_blocks - 1).reshape(
        local_heads, group_count, group_size, slot_count
    )

    def block_scores(query_group, grad_group, key_head, value_head, picks):
        key_blocks = key_head[picks]
        value_blocks = value_head[picks]
        scores = (
            jnp.einsum(
                "gbd,gskd->gbsk", query_group, key_blocks, preferred_element_type=jnp.float32
            )
            * scale
        )
        prod_grad = jnp.einsum(
            "gbd,gskd->gbsk", grad_group, value_blocks, preferred_element_type=jnp.float32
        )
        return (scores, prod_grad, key_blocks)

    def stats_head(head_inputs):
        query_head, grad_head, key_head, value_head, pick_head, live_head = head_inputs

        def stats_group(group_inputs):
            query_group, grad_group, picks, live_group = group_inputs
            scores, prod_grad, unused_keys = block_scores(
                query_group, grad_group, key_head, value_head, picks
            )
            live_mask = live_group[:, None, :, None]
            top_value = jnp.max(jnp.where(live_mask, scores, -1e30), axis=(2, 3))
            weight = jnp.where(live_mask, jnp.exp(scores - top_value[:, :, None, None]), 0.0)
            return (
                top_value,
                jnp.sum(weight, axis=(2, 3)),
                jnp.sum(weight * prod_grad, axis=(2, 3)),
            )

        return lax.map(stats_group, (query_head, grad_head, pick_head, live_head))

    top_value, total, weighted = lax.map(
        stats_head, (query_split, grad_split, key_split, value_split, slot_picks, live_slots)
    )
    top_value, total, weighted = joined((top_value, total, weighted), "memory", combine_stats)
    log_total = top_value + jnp.log(total)
    delta_row = weighted / total

    def grads_head(head_inputs):
        query_head, grad_head, key_head, value_head, pick_head, live_head, log_head, delta_head = (
            head_inputs
        )

        def grads_group(carry, group_inputs):
            query_group, grad_group, picks, live_group, log_group, delta_group = group_inputs
            scores, prod_grad, key_blocks = block_scores(
                query_group, grad_group, key_head, value_head, picks
            )
            live_mask = live_group[:, None, :, None]
            probs = jnp.where(live_mask, jnp.exp(scores - log_group[:, :, None, None]), 0.0)
            probs_half = probs.astype(jnp.bfloat16)
            score_grad = (probs * (prod_grad - delta_group[:, :, None, None])).astype(jnp.bfloat16)
            value_terms = jnp.einsum(
                "gbsk,gbd->gskd", probs_half, grad_group, preferred_element_type=jnp.float32
            )
            key_terms = (
                jnp.einsum(
                    "gbsk,gbd->gskd", score_grad, query_group, preferred_element_type=jnp.float32
                )
                * scale
            )
            query_terms = (
                jnp.einsum(
                    "gbsk,gskd->gbd", score_grad, key_blocks, preferred_element_type=jnp.float32
                )
                * scale
            )
            flat_picks = picks.reshape(-1)
            flat_live = live_group.reshape(-1)[:, None, None]
            key_total = (
                carry[0]
                .at[flat_picks]
                .add(jnp.where(flat_live, key_terms.reshape(-1, BLOCK, HEAD_DIM), 0.0))
            )
            value_total = (
                carry[1]
                .at[flat_picks]
                .add(jnp.where(flat_live, value_terms.reshape(-1, BLOCK, HEAD_DIM), 0.0))
            )
            return ((key_total, value_total), query_terms)

        zero_grad = jnp.zeros((memory_blocks, BLOCK, HEAD_DIM), jnp.float32)
        totals, query_terms = lax.scan(
            grads_group,
            (zero_grad, zero_grad),
            (query_head, grad_head, pick_head, live_head, log_head, delta_head),
        )
        return (query_terms, totals[0], totals[1])

    query_grad, key_grad, value_grad = lax.map(
        grads_head,
        (
            query_split,
            grad_split,
            key_split,
            value_split,
            slot_picks,
            live_slots,
            log_total,
            delta_row,
        ),
    )
    query_grad = query_grad.transpose(1, 2, 3, 0, 4).reshape(row_count, local_heads * HEAD_DIM)
    key_grad = key_grad.transpose(1, 2, 0, 3).reshape(memory_blocks * BLOCK, local_heads * HEAD_DIM)
    value_grad = value_grad.transpose(1, 2, 0, 3).reshape(
        memory_blocks * BLOCK, local_heads * HEAD_DIM
    )
    return (query_grad, key_grad, value_grad)


def span_shards(queries, keys, values, grad_out, blocks):
    query_span, grad_span = (
        lax.all_gather(queries, "memory", axis=0, tiled=True),
        lax.all_gather(grad_out, "memory", axis=0, tiled=True),
    )
    query_index = lax.axis_index("query")
    memory_index = lax.axis_index("memory")
    key_rows, value_rows = (
        lax.all_gather(keys, "query", axis=1, tiled=True),
        lax.all_gather(values, "query", axis=1, tiled=True),
    )
    span_blocks = query_span.shape[0] // BLOCK
    head_blocks = lax.dynamic_slice_in_dim(blocks, query_index * span_blocks, span_blocks, 1)
    query_part, key_full, value_full = local_grads(
        query_span, grad_span, key_rows, value_rows, head_blocks, memory_index
    )
    key_grad, value_grad = (
        lax.psum_scatter(key_full, "query", scatter_dimension=1, tiled=True),
        lax.psum_scatter(value_full, "query", scatter_dimension=1, tiled=True),
    )
    grad_query = lax.psum_scatter(
        query_part.astype(jnp.bfloat16), "memory", scatter_dimension=0, tiled=True
    )
    return (grad_query, key_grad.astype(jnp.bfloat16), value_grad.astype(jnp.bfloat16))


MESH = pl.DeviceIdType.MESH
NT = (((1,), (1,)), ((), ()))
TN = (((0,), (0,)), ((), ()))


def position():
    memory_size = lax.axis_size("memory")
    here = lax.axis_index("query") * memory_size + lax.axis_index("memory")
    return lax.axis_index("group"), here, memory_size


def meet(group, here, devices, memory_size):
    barrier = pltpu.get_barrier_semaphore()
    for step in range(1, devices):
        peer = lax.rem(here + step, devices)
        pl.semaphore_signal(
            barrier,
            inc=1,
            device_id=(group, peer // memory_size, lax.rem(peer, memory_size)),
            device_id_type=MESH,
        )
    pl.semaphore_wait(barrier, devices - 1)


def columns(index):
    return pl.ds(pl.multiple_of(index * HEAD_DIM, HEAD_DIM), HEAD_DIM)


def rows(index, size):
    return pl.ds(pl.multiple_of(index * size, size), size)


def to_heads_kernel(
    devices, query_ref, grad_ref, key_ref, value_ref, query_out, grad_out, key_out, value_out,
    send_sem, recv_sem, own_sem,
):
    group, here, memory_size = position()
    my_query, my_memory = here // memory_size, lax.rem(here, memory_size)
    row_count, memory_rows = query_ref.shape[0], key_ref.shape[0]
    meet(group, here, devices, memory_size)
    copies = []
    for step in range(1, memory_size):
        peer = lax.rem(my_memory + step, memory_size)
        for which, (source, target) in enumerate(((key_ref, key_out), (value_ref, value_out))):
            slot = 2 * devices + which * memory_size + step
            copy = pltpu.make_async_remote_copy(
                src_ref=source.at[:, columns(peer)],
                dst_ref=target.at[rows(my_memory, memory_rows), :],
                send_sem=send_sem.at[slot],
                recv_sem=recv_sem.at[slot],
                device_id=(group, my_query, peer),
                device_id_type=MESH,
            )
            copy.start()
            copies.append(copy)
    for step in range(1, devices):
        peer = lax.rem(here + step, devices)
        for which, (source, target) in enumerate(((query_ref, query_out), (grad_ref, grad_out))):
            slot = which * devices + step
            copy = pltpu.make_async_remote_copy(
                src_ref=source.at[:, columns(peer)],
                dst_ref=target.at[rows(here, row_count), :],
                send_sem=send_sem.at[slot],
                recv_sem=recv_sem.at[slot],
                device_id=(group, peer // memory_size, lax.rem(peer, memory_size)),
                device_id_type=MESH,
            )
            copy.start()
            copies.append(copy)
    own = [
        pltpu.make_async_copy(
            query_ref.at[:, columns(here)], query_out.at[rows(here, row_count), :], own_sem.at[0]
        ),
        pltpu.make_async_copy(
            grad_ref.at[:, columns(here)], grad_out.at[rows(here, row_count), :], own_sem.at[1]
        ),
        pltpu.make_async_copy(
            key_ref.at[:, columns(my_memory)], key_out.at[rows(my_memory, memory_rows), :], own_sem.at[2]
        ),
        pltpu.make_async_copy(
            value_ref.at[:, columns(my_memory)], value_out.at[rows(my_memory, memory_rows), :], own_sem.at[3]
        ),
    ]
    for copy in own:
        copy.start()
    for copy in own:
        copy.wait()
    for copy in copies:
        copy.wait()


def from_heads_kernel(
    devices, query_ref, key_ref, value_ref, query_out, key_out, value_out,
    send_sem, recv_sem, own_sem,
):
    group, here, memory_size = position()
    my_query, my_memory = here // memory_size, lax.rem(here, memory_size)
    row_count, memory_rows = query_out.shape[0], key_out.shape[0]
    meet(group, here, devices, memory_size)
    copies = []
    for step in range(1, memory_size):
        peer = lax.rem(my_memory + step, memory_size)
        for which, (source, target) in enumerate(((key_ref, key_out), (value_ref, value_out))):
            slot = devices + which * memory_size + step
            copy = pltpu.make_async_remote_copy(
                src_ref=source.at[rows(peer, memory_rows), :],
                dst_ref=target.at[:, columns(my_memory)],
                send_sem=send_sem.at[slot],
                recv_sem=recv_sem.at[slot],
                device_id=(group, my_query, peer),
                device_id_type=MESH,
            )
            copy.start()
            copies.append(copy)
    for step in range(1, devices):
        peer = lax.rem(here + step, devices)
        copy = pltpu.make_async_remote_copy(
            src_ref=query_ref.at[rows(peer, row_count), :],
            dst_ref=query_out.at[:, columns(here)],
            send_sem=send_sem.at[step],
            recv_sem=recv_sem.at[step],
            device_id=(group, peer // memory_size, lax.rem(peer, memory_size)),
            device_id_type=MESH,
        )
        copy.start()
        copies.append(copy)
    own = [
        pltpu.make_async_copy(
            query_ref.at[rows(here, row_count), :], query_out.at[:, columns(here)], own_sem.at[0]
        ),
        pltpu.make_async_copy(
            key_ref.at[rows(my_memory, memory_rows), :], key_out.at[:, columns(my_memory)], own_sem.at[1]
        ),
        pltpu.make_async_copy(
            value_ref.at[rows(my_memory, memory_rows), :], value_out.at[:, columns(my_memory)], own_sem.at[2]
        ),
    ]
    for copy in own:
        copy.start()
    for copy in own:
        copy.wait()
    for copy in copies:
        copy.wait()


def head_kernel(
    picks, query_ref, grad_ref, key_ref, value_ref, query_out, key_out, value_out,
    key_total, value_total,
):
    scale = 1.0 / math.sqrt(HEAD_DIM)
    key_total[...] = jnp.zeros_like(key_total)
    value_total[...] = jnp.zeros_like(value_total)

    def block(index, carry):
        here = rows(index, BLOCK)
        places = [rows(picks[index, slot], BLOCK) for slot in range(2)]
        query, grad = query_ref[here, :], grad_ref[here, :]
        keys = jnp.concatenate([key_ref[place, :] for place in places], axis=0)
        values = jnp.concatenate([value_ref[place, :] for place in places], axis=0)
        scores = lax.dot_general(query, keys, NT, preferred_element_type=jnp.float32) * scale
        prod_grad = lax.dot_general(grad, values, NT, preferred_element_type=jnp.float32)
        weight = jnp.exp(scores - jnp.max(scores, axis=1, keepdims=True))
        probs = weight / jnp.sum(weight, axis=1, keepdims=True)
        delta = jnp.sum(probs * prod_grad, axis=1, keepdims=True)
        probs_half = probs.astype(jnp.bfloat16)
        score_grad = (probs * (prod_grad - delta)).astype(jnp.bfloat16)
        query_out[here, :] = (
            lax.dot_general(
                score_grad, keys, (((1,), (0,)), ((), ())), preferred_element_type=jnp.float32
            )
            * scale
        ).astype(query_out.dtype)
        value_terms = lax.dot_general(probs_half, grad, TN, preferred_element_type=jnp.float32)
        key_terms = lax.dot_general(score_grad, query, TN, preferred_element_type=jnp.float32)
        for slot, place in enumerate(places):
            part = slice(slot * BLOCK, (slot + 1) * BLOCK)
            key_total[place, :] += key_terms[part]
            value_total[place, :] += value_terms[part]
        return carry

    lax.fori_loop(0, query_ref.shape[0] // BLOCK, block, 0, unroll=2)
    key_out[...] = (key_total[...] * scale).astype(key_out.dtype)
    value_out[...] = value_total[...].astype(value_out.dtype)


def head_shards(queries, keys, values, grad_out, blocks):
    memory_size = lax.axis_size("memory")
    devices = lax.axis_size("query") * memory_size
    row_count, memory_rows = queries.shape[0], keys.shape[0]
    all_rows, all_memory = row_count * devices, memory_rows * memory_size
    anywhere, vmem = pl.BlockSpec(memory_space=pl.ANY), pl.BlockSpec(memory_space=pltpu.VMEM)

    def like(*shape):
        return jax.ShapeDtypeStruct(shape, jnp.bfloat16)

    def semaphores(count, own):
        return [
            pltpu.SemaphoreType.DMA((count,)),
            pltpu.SemaphoreType.DMA((count,)),
            pltpu.SemaphoreType.DMA((own,)),
        ]

    query_head, grad_head, key_head, value_head = pl.pallas_call(
        functools.partial(to_heads_kernel, devices),
        out_shape=(
            like(all_rows, HEAD_DIM),
            like(all_rows, HEAD_DIM),
            like(all_memory, HEAD_DIM),
            like(all_memory, HEAD_DIM),
        ),
        in_specs=[anywhere] * 4,
        out_specs=(anywhere,) * 4,
        scratch_shapes=semaphores(2 * devices + 2 * memory_size, 4),
        compiler_params=pltpu.CompilerParams(collective_id=0, has_side_effects=True),
        name="to_heads",
    )(queries, grad_out, keys, values)
    head = lax.axis_index("query") * memory_size + lax.axis_index("memory")
    picks = lax.dynamic_index_in_dim(blocks, head, 0, keepdims=False)
    query_grad, key_grad, value_grad = pl.pallas_call(
        head_kernel,
        out_shape=(
            like(all_rows, HEAD_DIM),
            like(all_memory, HEAD_DIM),
            like(all_memory, HEAD_DIM),
        ),
        in_specs=[pl.BlockSpec(memory_space=pltpu.SMEM)] + [vmem] * 4,
        out_specs=(vmem,) * 3,
        scratch_shapes=[pltpu.VMEM((all_memory, HEAD_DIM), jnp.float32)] * 2,
        compiler_params=pltpu.CompilerParams(vmem_limit_bytes=32 * 1024 * 1024),
        name="head_grads",
    )(picks, query_head, grad_head, key_head, value_head)
    return pl.pallas_call(
        functools.partial(from_heads_kernel, devices),
        out_shape=(
            like(row_count, queries.shape[1]),
            like(memory_rows, keys.shape[1]),
            like(memory_rows, keys.shape[1]),
        ),
        in_specs=[anywhere] * 3,
        out_specs=(anywhere,) * 3,
        scratch_shapes=semaphores(devices + 2 * memory_size, 3),
        compiler_params=pltpu.CompilerParams(collective_id=1, has_side_effects=True),
        name="from_heads",
    )(query_grad, key_grad, value_grad)


def shards(queries, keys, values, grad_out, blocks):
    devices = lax.axis_size("query") * lax.axis_size("memory")
    if devices == blocks.shape[0]:
        return head_shards(queries, keys, values, grad_out, blocks)
    return span_shards(queries, keys, values, grad_out, blocks)


def solution(mesh):
    placed = (
        P(("group", "query", "memory"), None),
        P(("group", "memory"), "query"),
        P(("group", "memory"), "query"),
        P(("group", "query", "memory"), None),
        P(None, "group", None),
    )
    return jax.shard_map(
        shards,
        mesh=mesh,
        in_specs=placed,
        out_specs=(
            P(("group", "query", "memory"), None),
            P(("group", "memory"), "query"),
            P(("group", "memory"), "query"),
        ),
        check_vma=False,
    )
```

```python
import functools
import math

import jax
import jax.numpy as jnp
from jax import lax
from jax.experimental import pallas as pl
from jax.experimental.pallas import tpu as pltpu
from jax.sharding import PartitionSpec as P

HEAD_DIM = 128
BLOCK = 128


def joined(value, axis, combine):
    everything = jax.tree.map(lambda part: lax.all_gather(part, axis), value)
    leading = jax.tree.map(lambda part: part[0], everything)

    def hop(k, so_far):
        return combine(so_far, jax.tree.map(lambda part: part[k], everything))

    return lax.fori_loop(1, lax.axis_size(axis), hop, leading)


def combine_stats(first, second):
    top_value = jnp.maximum(first[0], second[0])
    first_factor = jnp.exp(first[0] - top_value)
    second_factor = jnp.exp(second[0] - top_value)
    return (
        top_value,
        first[1] * first_factor + second[1] * second_factor,
        first[2] * first_factor + second[2] * second_factor,
    )


def local_grads(query_rows, grad_rows, key_rows, value_rows, head_blocks, shard_index):
    row_count = query_rows.shape[0]
    query_blocks = row_count // BLOCK
    local_heads = query_rows.shape[1] // HEAD_DIM
    memory_blocks = key_rows.shape[0] // BLOCK
    slot_count = head_blocks.shape[2]
    group_size = math.gcd(query_blocks, 8)
    group_count = query_blocks // group_size
    scale = 1.0 / math.sqrt(HEAD_DIM)

    def split_queries(array):
        return array.reshape(group_count, group_size, BLOCK, local_heads, HEAD_DIM).transpose(
            3, 0, 1, 2, 4
        )

    def split_memory(array):
        return array.reshape(memory_blocks, BLOCK, local_heads, HEAD_DIM).transpose(2, 0, 1, 3)

    query_split = split_queries(query_rows)
    grad_split = split_queries(grad_rows)
    key_split = split_memory(key_rows)
    value_split = split_memory(value_rows)
    local_ids = head_blocks - shard_index * memory_blocks
    live_slots = ((local_ids >= 0) & (local_ids < memory_blocks)).reshape(
        local_heads, group_count, group_size, slot_count
    )
    slot_picks = jnp.clip(local_ids, 0, memory_blocks - 1).reshape(
        local_heads, group_count, group_size, slot_count
    )

    def block_scores(query_group, grad_group, key_head, value_head, picks):
        key_blocks = key_head[picks]
        value_blocks = value_head[picks]
        scores = (
            jnp.einsum(
                "gbd,gskd->gbsk", query_group, key_blocks, preferred_element_type=jnp.float32
            )
            * scale
        )
        prod_grad = jnp.einsum(
            "gbd,gskd->gbsk", grad_group, value_blocks, preferred_element_type=jnp.float32
        )
        return (scores, prod_grad, key_blocks)

    def stats_head(head_inputs):
        query_head, grad_head, key_head, value_head, pick_head, live_head = head_inputs

        def stats_group(group_inputs):
            query_group, grad_group, picks, live_group = group_inputs
            scores, prod_grad, unused_keys = block_scores(
                query_group, grad_group, key_head, value_head, picks
            )
            live_mask = live_group[:, None, :, None]
            top_value = jnp.max(jnp.where(live_mask, scores, -1e30), axis=(2, 3))
            weight = jnp.where(live_mask, jnp.exp(scores - top_value[:, :, None, None]), 0.0)
            return (
                top_value,
                jnp.sum(weight, axis=(2, 3)),
                jnp.sum(weight * prod_grad, axis=(2, 3)),
            )

        return lax.map(stats_group, (query_head, grad_head, pick_head, live_head))

    top_value, total, weighted = lax.map(
        stats_head, (query_split, grad_split, key_split, value_split, slot_picks, live_slots)
    )
    top_value, total, weighted = joined((top_value, total, weighted), "memory", combine_stats)
    log_total = top_value + jnp.log(total)
    delta_row = weighted / total

    def grads_head(head_inputs):
        query_head, grad_head, key_head, value_head, pick_head, live_head, log_head, delta_head = (
            head_inputs
        )

        def grads_group(carry, group_inputs):
            query_group, grad_group, picks, live_group, log_group, delta_group = group_inputs
            scores, prod_grad, key_blocks = block_scores(
                query_group, grad_group, key_head, value_head, picks
            )
            live_mask = live_group[:, None, :, None]
            probs = jnp.where(live_mask, jnp.exp(scores - log_group[:, :, None, None]), 0.0)
            probs_half = probs.astype(jnp.bfloat16)
            score_grad = (probs * (prod_grad - delta_group[:, :, None, None])).astype(jnp.bfloat16)
            value_terms = jnp.einsum(
                "gbsk,gbd->gskd", probs_half, grad_group, preferred_element_type=jnp.float32
            )
            key_terms = (
                jnp.einsum(
                    "gbsk,gbd->gskd", score_grad, query_group, preferred_element_type=jnp.float32
                )
                * scale
            )
            query_terms = (
                jnp.einsum(
                    "gbsk,gskd->gbd", score_grad, key_blocks, preferred_element_type=jnp.float32
                )
                * scale
            )
            flat_picks = picks.reshape(-1)
            flat_live = live_group.reshape(-1)[:, None, None]
            key_total = (
                carry[0]
                .at[flat_picks]
                .add(jnp.where(flat_live, key_terms.reshape(-1, BLOCK, HEAD_DIM), 0.0))
            )
            value_total = (
                carry[1]
                .at[flat_picks]
                .add(jnp.where(flat_live, value_terms.reshape(-1, BLOCK, HEAD_DIM), 0.0))
            )
            return ((key_total, value_total), query_terms)

        zero_grad = jnp.zeros((memory_blocks, BLOCK, HEAD_DIM), jnp.float32)
        totals, query_terms = lax.scan(
            grads_group,
            (zero_grad, zero_grad),
            (query_head, grad_head, pick_head, live_head, log_head, delta_head),
        )
        return (query_terms, totals[0], totals[1])

    query_grad, key_grad, value_grad = lax.map(
        grads_head,
        (
            query_split,
            grad_split,
            key_split,
            value_split,
            slot_picks,
            live_slots,
            log_total,
            delta_row,
        ),
    )
    query_grad = query_grad.transpose(1, 2, 3, 0, 4).reshape(row_count, local_heads * HEAD_DIM)
    key_grad = key_grad.transpose(1, 2, 0, 3).reshape(memory_blocks * BLOCK, local_heads * HEAD_DIM)
    value_grad = value_grad.transpose(1, 2, 0, 3).reshape(
        memory_blocks * BLOCK, local_heads * HEAD_DIM
    )
    return (query_grad, key_grad, value_grad)


def span_shards(queries, keys, values, grad_out, blocks):
    query_span, grad_span = (
        lax.all_gather(queries, "memory", axis=0, tiled=True),
        lax.all_gather(grad_out, "memory", axis=0, tiled=True),
    )
    query_index = lax.axis_index("query")
    memory_index = lax.axis_index("memory")
    key_rows, value_rows = (
        lax.all_gather(keys, "query", axis=1, tiled=True),
        lax.all_gather(values, "query", axis=1, tiled=True),
    )
    span_blocks = query_span.shape[0] // BLOCK
    head_blocks = lax.dynamic_slice_in_dim(blocks, query_index * span_blocks, span_blocks, 1)
    query_part, key_full, value_full = local_grads(
        query_span, grad_span, key_rows, value_rows, head_blocks, memory_index
    )
    key_grad, value_grad = (
        lax.psum_scatter(key_full, "query", scatter_dimension=1, tiled=True),
        lax.psum_scatter(value_full, "query", scatter_dimension=1, tiled=True),
    )
    grad_query = lax.psum_scatter(
        query_part.astype(jnp.bfloat16), "memory", scatter_dimension=0, tiled=True
    )
    return (grad_query, key_grad.astype(jnp.bfloat16), value_grad.astype(jnp.bfloat16))


MESH = pl.DeviceIdType.MESH
NT = (((1,), (1,)), ((), ()))
TN = (((0,), (0,)), ((), ()))
UNROLL = 2


def position():
    memory_size = lax.axis_size("memory")
    here = lax.axis_index("query") * memory_size + lax.axis_index("memory")
    return lax.axis_index("group"), here, memory_size


def meet(group, here, devices, memory_size):
    barrier = pltpu.get_barrier_semaphore()
    for step in range(1, devices):
        peer = lax.rem(here + step, devices)
        pl.semaphore_signal(
            barrier,
            inc=1,
            device_id=(group, peer // memory_size, lax.rem(peer, memory_size)),
            device_id_type=MESH,
        )
    pl.semaphore_wait(barrier, devices - 1)


def columns(index, width):
    return pl.ds(pl.multiple_of(index * width, width), width)


def rows(index, size):
    return pl.ds(pl.multiple_of(index * size, size), size)


def send_all(copies, own):
    for copy in copies + own:
        copy.start()
    for copy in own + copies:
        copy.wait()


def to_heads_kernel(
    devices, half, query_ref, grad_ref, key_ref, value_ref, query_out, grad_out, key_out, value_out,
    send_sem, recv_sem, own_sem,
):
    group, here, memory_size = position()
    my_query, my_memory = here // memory_size, lax.rem(here, memory_size)
    row_count, memory_rows = query_ref.shape[0], key_ref.shape[0]
    width = query_out.shape[1]
    base, lane = my_memory // half * half, lax.rem(my_memory, half)
    meet(group, here, devices, memory_size)
    copies, own = [], []
    for which, (source, target) in enumerate(((key_ref, key_out), (value_ref, value_out))):
        for step in range(half):
            peer = lax.rem(lane + step, half)
            slot = 2 * devices + which * half + step
            ends = dict(
                src_ref=source.at[:, columns(peer, width)],
                dst_ref=target.at[rows(lane, memory_rows), :],
            )
            if step == 0:
                own.append(pltpu.make_async_copy(*ends.values(), own_sem.at[which]))
            else:
                copies.append(
                    pltpu.make_async_remote_copy(
                        **ends,
                        send_sem=send_sem.at[slot],
                        recv_sem=recv_sem.at[slot],
                        device_id=(group, my_query, base + peer),
                        device_id_type=MESH,
                    )
                )
    for step in range(devices):
        peer = lax.rem(here + step, devices)
        peer_query, peer_memory = peer // memory_size, lax.rem(peer, memory_size)
        part = peer_query * half + lax.rem(peer_memory, half)
        for which, (source, target) in enumerate(((query_ref, query_out), (grad_ref, grad_out))):
            slot = which * devices + step
            ends = dict(
                src_ref=source.at[:, columns(part, width)],
                dst_ref=target.at[rows(here, row_count), :],
            )
            if step == 0:
                own.append(pltpu.make_async_copy(*ends.values(), own_sem.at[2 + which]))
            else:
                copies.append(
                    pltpu.make_async_remote_copy(
                        **ends,
                        send_sem=send_sem.at[slot],
                        recv_sem=recv_sem.at[slot],
                        device_id=(group, peer_query, peer_memory),
                        device_id_type=MESH,
                    )
                )
    send_all(copies, own)


def from_heads_kernel(
    devices, half, query_ref, key_ref, value_ref, query_out, key_out, value_out, parts,
    send_sem, recv_sem, own_sem,
):
    group, here, memory_size = position()
    my_query, my_memory = here // memory_size, lax.rem(here, memory_size)
    row_count, memory_rows = query_out.shape[0], key_out.shape[0]
    width = query_ref.shape[1]
    side, lane = my_memory // half, lax.rem(my_memory, half)
    meet(group, here, devices, memory_size)
    copies, own = [], []
    for which, (source, target) in enumerate(((key_ref, key_out), (value_ref, value_out))):
        for step in range(half):
            peer = lax.rem(lane + step, half)
            slot = devices + which * half + step
            ends = dict(
                src_ref=source.at[rows(peer, memory_rows), :],
                dst_ref=target.at[:, columns(lane, width)],
            )
            if step == 0:
                own.append(pltpu.make_async_copy(*ends.values(), own_sem.at[which]))
            else:
                copies.append(
                    pltpu.make_async_remote_copy(
                        **ends,
                        send_sem=send_sem.at[slot],
                        recv_sem=recv_sem.at[slot],
                        device_id=(group, my_query, side * half + peer),
                        device_id_type=MESH,
                    )
                )
    for step in range(devices):
        peer = lax.rem(here + step, devices)
        ends = dict(
            src_ref=query_ref.at[rows(peer, row_count), :],
            dst_ref=parts.at[side, :, columns(my_query * half + lane, width)],
        )
        if step == 0:
            own.append(pltpu.make_async_copy(*ends.values(), own_sem.at[2]))
        else:
            copies.append(
                pltpu.make_async_remote_copy(
                    **ends,
                    send_sem=send_sem.at[step],
                    recv_sem=recv_sem.at[step],
                    device_id=(group, peer // memory_size, lax.rem(peer, memory_size)),
                    device_id_type=MESH,
                )
            )
    send_all(copies, own)
    total = parts[0].astype(jnp.float32) + parts[1].astype(jnp.float32)
    query_out[...] = total.astype(query_out.dtype)


def combine_kernel(half, stats_ref, out_ref, other, send_sem, recv_sem):
    group, here, memory_size = position()
    my_query, my_memory = here // memory_size, lax.rem(here, memory_size)
    partner = (group, my_query, lax.rem(my_memory + half, memory_size))
    barrier = pltpu.get_barrier_semaphore()
    pl.semaphore_signal(barrier, inc=1, device_id=partner, device_id_type=MESH)
    pl.semaphore_wait(barrier, 1)
    copy = pltpu.make_async_remote_copy(
        src_ref=stats_ref,
        dst_ref=other,
        send_sem=send_sem,
        recv_sem=recv_sem,
        device_id=partner,
        device_id_type=MESH,
    )
    copy.start()
    copy.wait()
    top, total, weighted = combine_stats(
        (stats_ref[0], stats_ref[1], stats_ref[2]), (other[0], other[1], other[2])
    )
    out_ref[0] = top + jnp.log(total)
    out_ref[1] = weighted / total


def list_live(picks, live, half_blocks):
    def add(number, count):
        live[count] = number
        pick = picks[number]
        return count + jnp.where((pick >= 0) & (pick < half_blocks), 1, 0)

    return lax.fori_loop(0, picks.shape[0], add, 0)


def pair_of(number, picks, query_blocks):
    row = number // 2
    head, block = row // query_blocks, lax.rem(row, query_blocks)
    return row, columns(head, HEAD_DIM), rows(block, BLOCK), rows(picks[number], BLOCK)


def pair_scores(query, grad, key, value):
    scale = 1.0 / math.sqrt(HEAD_DIM)
    scores = lax.dot_general(key, query, NT, preferred_element_type=jnp.float32) * scale
    prod_grad = lax.dot_general(value, grad, NT, preferred_element_type=jnp.float32)
    return scores, prod_grad


def stats_kernel(picks, query_ref, grad_ref, key_ref, value_ref, out_ref, parts, live):
    query_blocks = query_ref.shape[0] // BLOCK
    parts[:, 0] = jnp.full(parts[:, 0].shape, -1e30, jnp.float32)
    parts[:, 1:] = jnp.zeros(parts[:, 1:].shape, jnp.float32)
    count = list_live(picks, live, key_ref.shape[0] // BLOCK)

    def step(index, carry):
        for part in range(UNROLL):
            number = live[jnp.minimum(index * UNROLL + part, count - 1)]
            row, head, here, there = pair_of(number, picks, query_blocks)
            scores, prod_grad = pair_scores(
                query_ref[here, head], grad_ref[here, head], key_ref[there, head], value_ref[there, head]
            )
            top = jnp.max(scores, axis=0, keepdims=True)
            weight = jnp.exp(scores - top)
            slot, line = lax.rem(number, 2), pl.ds(row, 1)
            parts[slot, 0, line, :] = top
            parts[slot, 1, line, :] = jnp.sum(weight, axis=0, keepdims=True)
            parts[slot, 2, line, :] = jnp.sum(weight * prod_grad, axis=0, keepdims=True)
        return carry

    lax.fori_loop(0, (count + UNROLL - 1) // UNROLL, step, 0)
    both = combine_stats(
        (parts[0, 0], parts[0, 1], parts[0, 2]), (parts[1, 0], parts[1, 1], parts[1, 2])
    )
    for index in range(3):
        out_ref[index] = both[index]


def grads_kernel(
    picks, stats_ref, query_ref, grad_ref, key_ref, value_ref, query_out, key_out, value_out,
    query_total, key_total, value_total, live,
):
    scale = 1.0 / math.sqrt(HEAD_DIM)
    query_blocks = query_ref.shape[0] // BLOCK
    for total in (query_total, key_total, value_total):
        total[...] = jnp.zeros_like(total)
    count = list_live(picks, live, key_ref.shape[0] // BLOCK)

    def step(index, carry):
        terms = []
        for part in range(UNROLL):
            at = index * UNROLL + part
            number = live[jnp.minimum(at, count - 1)]
            row, head, here, there = pair_of(number, picks, query_blocks)
            query, grad, key = query_ref[here, head], grad_ref[here, head], key_ref[there, head]
            scores, prod_grad = pair_scores(query, grad, key, value_ref[there, head])
            line = pl.ds(row, 1)
            probs = jnp.exp(scores - stats_ref[0, line, :])
            probs = jnp.where(at < count, probs, 0.0)
            probs_half = probs.astype(jnp.bfloat16)
            score_grad = (probs * (prod_grad - stats_ref[1, line, :])).astype(jnp.bfloat16)
            plain = (((1,), (0,)), ((), ()))
            terms.append((
                head, here, there,
                lax.dot_general(probs_half, grad, plain, preferred_element_type=jnp.float32),
                lax.dot_general(score_grad, query, plain, preferred_element_type=jnp.float32),
                lax.dot_general(score_grad, key, TN, preferred_element_type=jnp.float32),
            ))
        for head, here, there, value_term, key_term, query_term in terms:
            value_total[there, head] += value_term
            key_total[there, head] += key_term
            query_total[here, head] += query_term
        return carry

    lax.fori_loop(0, (count + UNROLL - 1) // UNROLL, step, 0)
    query_out[...] = (query_total[...] * scale).astype(query_out.dtype)
    key_out[...] = (key_total[...] * scale).astype(key_out.dtype)
    value_out[...] = value_total[...].astype(value_out.dtype)


def head_shards(queries, keys, values, grad_out, blocks):
    memory_size = lax.axis_size("memory")
    devices = lax.axis_size("query") * memory_size
    half = memory_size // 2
    row_count, memory_rows = queries.shape[0], keys.shape[0]
    all_rows, half_rows = row_count * devices, memory_rows * half
    width = keys.shape[1] // half
    heads = width // HEAD_DIM
    stat_rows, pairs = heads * all_rows // BLOCK, 2 * heads * all_rows // BLOCK
    anywhere, vmem = pl.BlockSpec(memory_space=pl.ANY), pl.BlockSpec(memory_space=pltpu.VMEM)
    smem = pl.BlockSpec(memory_space=pltpu.SMEM)
    local = pltpu.CompilerParams(vmem_limit_bytes=40 * 1024 * 1024)

    def like(*shape, dtype=jnp.bfloat16):
        return jax.ShapeDtypeStruct(shape, dtype)

    def semaphores(count, own):
        return [
            pltpu.SemaphoreType.DMA((count,)),
            pltpu.SemaphoreType.DMA((count,)),
            pltpu.SemaphoreType.DMA((own,)),
        ]

    def remote(number):
        return pltpu.CompilerParams(
            collective_id=number, has_side_effects=True, vmem_limit_bytes=40 * 1024 * 1024
        )

    arrays = pl.pallas_call(
        functools.partial(to_heads_kernel, devices, half),
        out_shape=(
            like(all_rows, width), like(all_rows, width),
            like(half_rows, width), like(half_rows, width),
        ),
        in_specs=[anywhere] * 4,
        out_specs=(anywhere,) * 4,
        scratch_shapes=semaphores(2 * devices + 2 * half, 4),
        compiler_params=remote(0),
        name="to_heads",
    )(queries, grad_out, keys, values)
    my_query, my_memory = lax.axis_index("query"), lax.axis_index("memory")
    first_head = (my_query * half + my_memory % half) * heads
    picks = lax.dynamic_slice_in_dim(blocks, first_head, heads, 0).reshape(pairs)
    picks = picks - my_memory // half * (half_rows // BLOCK)
    stats = pl.pallas_call(
        stats_kernel,
        out_shape=like(3, stat_rows, BLOCK, dtype=jnp.float32),
        in_specs=[smem] + [vmem] * 4,
        out_specs=vmem,
        scratch_shapes=[
            pltpu.VMEM((2, 3, stat_rows, BLOCK), jnp.float32),
            pltpu.SMEM((pairs,), jnp.int32),
        ],
        compiler_params=local,
        name="stats",
    )(picks, *arrays)
    stats = pl.pallas_call(
        functools.partial(combine_kernel, half),
        out_shape=like(2, stat_rows, BLOCK, dtype=jnp.float32),
        in_specs=[vmem],
        out_specs=vmem,
        scratch_shapes=[
            pltpu.VMEM((3, stat_rows, BLOCK), jnp.float32),
            pltpu.SemaphoreType.DMA,
            pltpu.SemaphoreType.DMA,
        ],
        compiler_params=remote(1),
        name="combine",
    )(stats)
    grads = pl.pallas_call(
        grads_kernel,
        out_shape=(like(all_rows, width), like(half_rows, width), like(half_rows, width)),
        in_specs=[smem] + [vmem] * 5,
        out_specs=(vmem,) * 3,
        scratch_shapes=[
            pltpu.VMEM((all_rows, width), jnp.float32),
            pltpu.VMEM((half_rows, width), jnp.float32),
            pltpu.VMEM((half_rows, width), jnp.float32),
            pltpu.SMEM((pairs,), jnp.int32),
        ],
        compiler_params=local,
        name="head_grads",
    )(picks, stats, *arrays)
    return pl.pallas_call(
        functools.partial(from_heads_kernel, devices, half),
        out_shape=(
            like(row_count, queries.shape[1]),
            like(memory_rows, keys.shape[1]),
            like(memory_rows, keys.shape[1]),
        ),
        in_specs=[anywhere] * 3,
        out_specs=(vmem, anywhere, anywhere),
        scratch_shapes=[pltpu.VMEM((2, row_count, queries.shape[1]), jnp.bfloat16)]
        + semaphores(devices + 2 * half, 3),
        compiler_params=remote(2),
        name="from_heads",
    )(*grads)


def shards(queries, keys, values, grad_out, blocks):
    memory_size = lax.axis_size("memory")
    whole_heads = keys.shape[1] % (memory_size // 2 * HEAD_DIM) == 0
    if memory_size % 2 == 0 and whole_heads and blocks.shape[2] == 2:
        return head_shards(queries, keys, values, grad_out, blocks)
    return span_shards(queries, keys, values, grad_out, blocks)


def solution(mesh):
    placed = (
        P(("group", "query", "memory"), None),
        P(("group", "memory"), "query"),
        P(("group", "memory"), "query"),
        P(("group", "query", "memory"), None),
        P(None, "group", None),
    )
    return jax.shard_map(
        shards,
        mesh=mesh,
        in_specs=placed,
        out_specs=(
            P(("group", "query", "memory"), None),
            P(("group", "memory"), "query"),
            P(("group", "memory"), "query"),
        ),
        check_vma=False,
    )
```

```python
import functools
import math

import jax
import jax.numpy as jnp
from jax import lax
from jax.experimental import pallas as pl
from jax.experimental.pallas import tpu as pltpu
from jax.sharding import PartitionSpec as P

HEAD_DIM = 128
BLOCK = 128


def joined(value, axis, combine):
    everything = jax.tree.map(lambda part: lax.all_gather(part, axis), value)
    leading = jax.tree.map(lambda part: part[0], everything)

    def hop(k, so_far):
        return combine(so_far, jax.tree.map(lambda part: part[k], everything))

    return lax.fori_loop(1, lax.axis_size(axis), hop, leading)


def combine_stats(first, second):
    top_value = jnp.maximum(first[0], second[0])
    first_factor = jnp.exp(first[0] - top_value)
    second_factor = jnp.exp(second[0] - top_value)
    return (
        top_value,
        first[1] * first_factor + second[1] * second_factor,
        first[2] * first_factor + second[2] * second_factor,
    )


def local_grads(query_rows, grad_rows, key_rows, value_rows, head_blocks, shard_index):
    row_count = query_rows.shape[0]
    query_blocks = row_count // BLOCK
    local_heads = query_rows.shape[1] // HEAD_DIM
    memory_blocks = key_rows.shape[0] // BLOCK
    slot_count = head_blocks.shape[2]
    group_size = math.gcd(query_blocks, 8)
    group_count = query_blocks // group_size
    scale = 1.0 / math.sqrt(HEAD_DIM)

    def split_queries(array):
        return array.reshape(group_count, group_size, BLOCK, local_heads, HEAD_DIM).transpose(
            3, 0, 1, 2, 4
        )

    def split_memory(array):
        return array.reshape(memory_blocks, BLOCK, local_heads, HEAD_DIM).transpose(2, 0, 1, 3)

    query_split = split_queries(query_rows)
    grad_split = split_queries(grad_rows)
    key_split = split_memory(key_rows)
    value_split = split_memory(value_rows)
    local_ids = head_blocks - shard_index * memory_blocks
    live_slots = ((local_ids >= 0) & (local_ids < memory_blocks)).reshape(
        local_heads, group_count, group_size, slot_count
    )
    slot_picks = jnp.clip(local_ids, 0, memory_blocks - 1).reshape(
        local_heads, group_count, group_size, slot_count
    )

    def block_scores(query_group, grad_group, key_head, value_head, picks):
        key_blocks = key_head[picks]
        value_blocks = value_head[picks]
        scores = (
            jnp.einsum(
                "gbd,gskd->gbsk", query_group, key_blocks, preferred_element_type=jnp.float32
            )
            * scale
        )
        prod_grad = jnp.einsum(
            "gbd,gskd->gbsk", grad_group, value_blocks, preferred_element_type=jnp.float32
        )
        return (scores, prod_grad, key_blocks)

    def stats_head(head_inputs):
        query_head, grad_head, key_head, value_head, pick_head, live_head = head_inputs

        def stats_group(group_inputs):
            query_group, grad_group, picks, live_group = group_inputs
            scores, prod_grad, unused_keys = block_scores(
                query_group, grad_group, key_head, value_head, picks
            )
            live_mask = live_group[:, None, :, None]
            top_value = jnp.max(jnp.where(live_mask, scores, -1e30), axis=(2, 3))
            weight = jnp.where(live_mask, jnp.exp(scores - top_value[:, :, None, None]), 0.0)
            return (
                top_value,
                jnp.sum(weight, axis=(2, 3)),
                jnp.sum(weight * prod_grad, axis=(2, 3)),
            )

        return lax.map(stats_group, (query_head, grad_head, pick_head, live_head))

    top_value, total, weighted = lax.map(
        stats_head, (query_split, grad_split, key_split, value_split, slot_picks, live_slots)
    )
    top_value, total, weighted = joined((top_value, total, weighted), "memory", combine_stats)
    log_total = top_value + jnp.log(total)
    delta_row = weighted / total

    def grads_head(head_inputs):
        query_head, grad_head, key_head, value_head, pick_head, live_head, log_head, delta_head = (
            head_inputs
        )

        def grads_group(carry, group_inputs):
            query_group, grad_group, picks, live_group, log_group, delta_group = group_inputs
            scores, prod_grad, key_blocks = block_scores(
                query_group, grad_group, key_head, value_head, picks
            )
            live_mask = live_group[:, None, :, None]
            probs = jnp.where(live_mask, jnp.exp(scores - log_group[:, :, None, None]), 0.0)
            probs_half = probs.astype(jnp.bfloat16)
            score_grad = (probs * (prod_grad - delta_group[:, :, None, None])).astype(jnp.bfloat16)
            value_terms = jnp.einsum(
                "gbsk,gbd->gskd", probs_half, grad_group, preferred_element_type=jnp.float32
            )
            key_terms = (
                jnp.einsum(
                    "gbsk,gbd->gskd", score_grad, query_group, preferred_element_type=jnp.float32
                )
                * scale
            )
            query_terms = (
                jnp.einsum(
                    "gbsk,gskd->gbd", score_grad, key_blocks, preferred_element_type=jnp.float32
                )
                * scale
            )
            flat_picks = picks.reshape(-1)
            flat_live = live_group.reshape(-1)[:, None, None]
            key_total = (
                carry[0]
                .at[flat_picks]
                .add(jnp.where(flat_live, key_terms.reshape(-1, BLOCK, HEAD_DIM), 0.0))
            )
            value_total = (
                carry[1]
                .at[flat_picks]
                .add(jnp.where(flat_live, value_terms.reshape(-1, BLOCK, HEAD_DIM), 0.0))
            )
            return ((key_total, value_total), query_terms)

        zero_grad = jnp.zeros((memory_blocks, BLOCK, HEAD_DIM), jnp.float32)
        totals, query_terms = lax.scan(
            grads_group,
            (zero_grad, zero_grad),
            (query_head, grad_head, pick_head, live_head, log_head, delta_head),
        )
        return (query_terms, totals[0], totals[1])

    query_grad, key_grad, value_grad = lax.map(
        grads_head,
        (
            query_split,
            grad_split,
            key_split,
            value_split,
            slot_picks,
            live_slots,
            log_total,
            delta_row,
        ),
    )
    query_grad = query_grad.transpose(1, 2, 3, 0, 4).reshape(row_count, local_heads * HEAD_DIM)
    key_grad = key_grad.transpose(1, 2, 0, 3).reshape(memory_blocks * BLOCK, local_heads * HEAD_DIM)
    value_grad = value_grad.transpose(1, 2, 0, 3).reshape(
        memory_blocks * BLOCK, local_heads * HEAD_DIM
    )
    return (query_grad, key_grad, value_grad)


def span_shards(queries, keys, values, grad_out, blocks):
    query_span, grad_span = (
        lax.all_gather(queries, "memory", axis=0, tiled=True),
        lax.all_gather(grad_out, "memory", axis=0, tiled=True),
    )
    query_index = lax.axis_index("query")
    memory_index = lax.axis_index("memory")
    key_rows, value_rows = (
        lax.all_gather(keys, "query", axis=1, tiled=True),
        lax.all_gather(values, "query", axis=1, tiled=True),
    )
    span_blocks = query_span.shape[0] // BLOCK
    head_blocks = lax.dynamic_slice_in_dim(blocks, query_index * span_blocks, span_blocks, 1)
    query_part, key_full, value_full = local_grads(
        query_span, grad_span, key_rows, value_rows, head_blocks, memory_index
    )
    key_grad, value_grad = (
        lax.psum_scatter(key_full, "query", scatter_dimension=1, tiled=True),
        lax.psum_scatter(value_full, "query", scatter_dimension=1, tiled=True),
    )
    grad_query = lax.psum_scatter(
        query_part.astype(jnp.bfloat16), "memory", scatter_dimension=0, tiled=True
    )
    return (grad_query, key_grad.astype(jnp.bfloat16), value_grad.astype(jnp.bfloat16))


MESH = pl.DeviceIdType.MESH
NT = (((1,), (1,)), ((), ()))
TN = (((0,), (0,)), ((), ()))
UNROLL = 2


def position():
    memory_size = lax.axis_size("memory")
    here = lax.axis_index("query") * memory_size + lax.axis_index("memory")
    return lax.axis_index("group"), here, memory_size


def meet(group, here, devices, memory_size):
    barrier = pltpu.get_barrier_semaphore()
    for step in range(1, devices):
        peer = lax.rem(here + step, devices)
        pl.semaphore_signal(
            barrier,
            inc=1,
            device_id=(group, peer // memory_size, lax.rem(peer, memory_size)),
            device_id_type=MESH,
        )
    pl.semaphore_wait(barrier, devices - 1)


def columns(index, width):
    return pl.ds(pl.multiple_of(index * width, width), width)


def rows(index, size):
    return pl.ds(pl.multiple_of(index * size, size), size)


def away(group, memory_size, peer):
    return (group, peer // memory_size, lax.rem(peer, memory_size))


def fused_kernel(
    devices, half, heads,
    picks, earlier, latest, live_ref, query_ref, grad_ref, key_ref, value_ref,
    query_out, key_out, value_out,
    query_in, grad_in, key_in, value_in, weights, products, stats, other, key_sums, value_sums,
    query_stage, key_stage, value_stage, parts,
    in_send, in_recv, in_own, stat_send, stat_recv, out_send, out_recv, out_own,
):
    scale = 1.0 / math.sqrt(HEAD_DIM)
    group, here, memory_size = position()
    my_query, my_memory = here // memory_size, lax.rem(here, memory_size)
    side, lane = my_memory // half, lax.rem(my_memory, half)
    partner = (group, my_query, lax.rem(my_memory + half, memory_size))
    row_count, own_blocks = query_ref.shape[0], key_ref.shape[0]
    memory_rows = own_blocks * BLOCK
    query_blocks = query_in.shape[1] // BLOCK
    half_blocks = key_in[0].shape[0]
    slots = 2 * query_blocks
    meet(group, here, devices, memory_size)

    def transfer(source, target, step, device, send, recv, own):
        if step == 0:
            return pltpu.make_async_copy(source, target, own)
        return pltpu.make_async_remote_copy(
            src_ref=source, dst_ref=target, send_sem=send, recv_sem=recv,
            device_id=device, device_id_type=MESH,
        )

    arrivals = []
    for head in range(heads):
        copies = []
        for which, (source, target) in enumerate(((key_ref, key_in), (value_ref, value_in))):
            for step in range(half):
                peer = lax.rem(lane + step, half)
                at = 2 * devices + which * half + step
                copies.append(transfer(
                    source.at[:, :, columns(peer * heads + head, HEAD_DIM)],
                    target[head].at[pl.ds(lane * own_blocks, own_blocks)],
                    step, (group, my_query, side * half + peer),
                    in_send.at[head, at], in_recv.at[head, at], in_own.at[head, which],
                ))
        for step in range(devices):
            peer = lax.rem(here + step, devices)
            first = (peer // memory_size * half + lax.rem(lax.rem(peer, memory_size), half)) * heads
            for which, (source, target) in enumerate(((query_ref, query_in), (grad_ref, grad_in))):
                at = which * devices + step
                copies.append(transfer(
                    source.at[:, columns(first + head, HEAD_DIM)],
                    target.at[head, rows(here, row_count), :],
                    step, away(group, memory_size, peer),
                    in_send.at[head, at], in_recv.at[head, at], in_own.at[head, 2 + which],
                ))
        for copy in copies:
            copy.start()
        arrivals.append(copies)

    key_sums[0] = jnp.zeros(key_sums.shape[1:], jnp.float32)
    value_sums[0] = jnp.zeros(value_sums.shape[1:], jnp.float32)
    returns = []
    for head in range(heads):
        for copy in arrivals[head]:
            copy.wait()

        def pick(block, slot):
            number = head * slots + 2 * block + slot
            return picks[number], live_ref[pl.ds(number, 1), :]

        def stats_step(block, carry):
            mine = rows(block, BLOCK)
            query, grad = query_in[head, mine, :], grad_in[head, mine, :]
            scores = []
            for slot in range(2):
                place, live = pick(block, slot)
                score = lax.dot_general(
                    key_in[head][place], query, NT, preferred_element_type=jnp.float32
                )
                scores.append(jnp.where(live > 0.0, score * scale, -1e30))
                products[2 * block + slot] = lax.dot_general(
                    value_in[head][place], grad, NT, preferred_element_type=jnp.float32
                )
            top = jnp.maximum(
                jnp.max(scores[0], axis=0, keepdims=True), jnp.max(scores[1], axis=0, keepdims=True)
            )
            total, weighted = 0.0, 0.0
            for slot in range(2):
                place, live = pick(block, slot)
                weight = jnp.exp(scores[slot] - top) * live
                weights[2 * block + slot] = weight
                total += jnp.sum(weight, axis=0, keepdims=True)
                weighted += jnp.sum(weight * products[2 * block + slot], axis=0, keepdims=True)
            line = pl.ds(block, 1)
            stats[head, 0, line, :] = top
            stats[head, 1, line, :] = total
            stats[head, 2, line, :] = weighted
            return carry

        lax.fori_loop(0, query_blocks, stats_step, 0, unroll=UNROLL)
        exchange = pltpu.make_async_remote_copy(
            src_ref=stats.at[head], dst_ref=other.at[head],
            send_sem=stat_send.at[head], recv_sem=stat_recv.at[head],
            device_id=partner, device_id_type=MESH,
        )
        exchange.start()
        exchange.wait()
        ours = (stats[head, 0], stats[head, 1], stats[head, 2])
        top, total, weighted = combine_stats(ours, (other[head, 0], other[head, 1], other[head, 2]))
        stats[head, 0] = jnp.exp(ours[0] - top) / total
        stats[head, 1] = weighted / total

        def grads_step(block, carry):
            mine, line = rows(block, BLOCK), pl.ds(block, 1)
            query, grad = query_in[head, mine, :], grad_in[head, mine, :]
            factor, delta = stats[head, 0, line, :], stats[head, 1, line, :]
            query_term = 0.0
            plain = (((1,), (0,)), ((), ()))
            key_terms, value_terms = [], []
            for slot in range(2):
                place, live = pick(block, slot)
                number = 2 * block + slot
                probs = weights[number] * factor
                score_grad = (probs * (products[number] - delta)).astype(jnp.bfloat16)
                value_terms.append(lax.dot_general(
                    probs.astype(jnp.bfloat16), grad, plain, preferred_element_type=jnp.float32
                ))
                key_terms.append(lax.dot_general(
                    score_grad, query, plain, preferred_element_type=jnp.float32
                ))
                query_term += lax.dot_general(
                    score_grad, key_in[head][place], TN, preferred_element_type=jnp.float32
                )
            query_stage[head, mine, :] = (query_term * scale).astype(query_stage.dtype)
            for slot in range(2):
                number = 2 * block + slot
                before = earlier[head * slots + number]
                key_sums[number + 1] = key_sums[before] + key_terms[slot]
                value_sums[number + 1] = value_sums[before] + value_terms[slot]
            return carry

        lax.fori_loop(0, query_blocks, grads_step, 0, unroll=UNROLL)

        def finish_step(block, carry):
            last = latest[head * half_blocks + block]
            mine = rows(block, BLOCK)
            key_stage[head, mine, :] = (key_sums[last] * scale).astype(key_stage.dtype)
            value_stage[head, mine, :] = value_sums[last].astype(value_stage.dtype)
            return carry

        lax.fori_loop(0, half_blocks, finish_step, 0, unroll=UNROLL)

        copies = []
        for which, (source, target) in enumerate(((key_stage, key_out), (value_stage, value_out))):
            for step in range(half):
                peer = lax.rem(lane + step, half)
                at = devices + which * half + step
                copies.append(transfer(
                    source.at[head, rows(peer, memory_rows), :],
                    target.at[:, columns(lane * heads + head, HEAD_DIM)],
                    step, (group, my_query, side * half + peer),
                    out_send.at[head, at], out_recv.at[head, at], out_own.at[head, which],
                ))
        for step in range(devices):
            peer = lax.rem(here + step, devices)
            copies.append(transfer(
                query_stage.at[head, rows(peer, row_count), :],
                parts.at[side, :, columns((my_query * half + lane) * heads + head, HEAD_DIM)],
                step, away(group, memory_size, peer),
                out_send.at[head, step], out_recv.at[head, step], out_own.at[head, 2],
            ))
        for copy in copies:
            copy.start()
        returns += copies

    for copy in returns:
        copy.wait()
    query_out[...] = (parts[0].astype(jnp.float32) + parts[1].astype(jnp.float32)).astype(
        query_out.dtype
    )


def head_shards(queries, keys, values, grad_out, blocks):
    memory_size = lax.axis_size("memory")
    devices = lax.axis_size("query") * memory_size
    half = memory_size // 2
    row_count, memory_rows = queries.shape[0], keys.shape[0]
    all_rows, half_rows = row_count * devices, memory_rows * half
    heads = keys.shape[1] // half // HEAD_DIM
    query_blocks, half_blocks = all_rows // BLOCK, half_rows // BLOCK
    slots = 2 * query_blocks
    anywhere, vmem = pl.BlockSpec(memory_space=pl.ANY), pl.BlockSpec(memory_space=pltpu.VMEM)
    smem = pl.BlockSpec(memory_space=pltpu.SMEM)

    my_query, my_memory = lax.axis_index("query"), lax.axis_index("memory")
    first_head = (my_query * half + my_memory % half) * heads
    picks = lax.dynamic_slice_in_dim(blocks, first_head, heads, 0).reshape(heads, slots)
    picks = picks - my_memory // half * half_blocks
    inside = (picks >= 0) & (picks < half_blocks)
    live = jnp.broadcast_to(inside.reshape(-1, 1), (heads * slots, BLOCK)).astype(jnp.float32)
    numbers = jnp.arange(slots, dtype=jnp.int32)
    same = (picks[:, :, None] == picks[:, None, :]) & (numbers[:, None] > numbers[None, :])
    earlier = jnp.max(jnp.where(same, numbers + 1, 0), axis=2)
    named = picks[:, None, :] == jnp.arange(half_blocks, dtype=jnp.int32)[:, None]
    latest = jnp.max(jnp.where(named, numbers + 1, 0), axis=2)

    places = jnp.clip(picks, 0, half_blocks - 1)

    def blocked(array):
        return array.reshape(-1, BLOCK, array.shape[1])

    def half_precision(*shape):
        return pltpu.VMEM(shape, jnp.bfloat16)

    def single_precision(*shape):
        return pltpu.VMEM(shape, jnp.float32)

    def semaphores(*shape):
        return pltpu.SemaphoreType.DMA(shape)

    arrivals, returns = 2 * devices + 2 * half, devices + 2 * half
    return pl.pallas_call(
        functools.partial(fused_kernel, devices, half, heads),
        out_shape=(
            jax.ShapeDtypeStruct(queries.shape, jnp.bfloat16),
            jax.ShapeDtypeStruct(keys.shape, jnp.bfloat16),
            jax.ShapeDtypeStruct(values.shape, jnp.bfloat16),
        ),
        in_specs=[smem] * 3 + [vmem] + [anywhere] * 4,
        out_specs=(vmem, anywhere, anywhere),
        scratch_shapes=[
            half_precision(heads, all_rows, HEAD_DIM),
            half_precision(heads, all_rows, HEAD_DIM),
            [half_precision(half_blocks, BLOCK, HEAD_DIM)] * heads,
            [half_precision(half_blocks, BLOCK, HEAD_DIM)] * heads,
            single_precision(slots, BLOCK, BLOCK),
            single_precision(slots, BLOCK, BLOCK),
            single_precision(heads, 3, query_blocks, BLOCK),
            single_precision(heads, 3, query_blocks, BLOCK),
            single_precision(slots + 1, BLOCK, HEAD_DIM),
            single_precision(slots + 1, BLOCK, HEAD_DIM),
            half_precision(heads, all_rows, HEAD_DIM),
            half_precision(heads, half_rows, HEAD_DIM),
            half_precision(heads, half_rows, HEAD_DIM),
            half_precision(2, row_count, queries.shape[1]),
            semaphores(heads, arrivals),
            semaphores(heads, arrivals),
            semaphores(heads, 4),
            semaphores(heads),
            semaphores(heads),
            semaphores(heads, returns),
            semaphores(heads, returns),
            semaphores(heads, 3),
        ],
        compiler_params=pltpu.CompilerParams(
            collective_id=0, has_side_effects=True, vmem_limit_bytes=48 * 1024 * 1024
        ),
        name="head_grads",
    )(
        places.reshape(-1), earlier.reshape(-1), latest.reshape(-1),
        live, queries, grad_out, blocked(keys), blocked(values),
    )


def shards(queries, keys, values, grad_out, blocks):
    memory_size = lax.axis_size("memory")
    whole_heads = keys.shape[1] % (memory_size // 2 * HEAD_DIM) == 0
    if memory_size % 2 == 0 and whole_heads and blocks.shape[2] == 2:
        return head_shards(queries, keys, values, grad_out, blocks)
    return span_shards(queries, keys, values, grad_out, blocks)


def solution(mesh):
    placed = (
        P(("group", "query", "memory"), None),
        P(("group", "memory"), "query"),
        P(("group", "memory"), "query"),
        P(("group", "query", "memory"), None),
        P(None, "group", None),
    )
    return jax.shard_map(
        shards,
        mesh=mesh,
        in_specs=placed,
        out_specs=(
            P(("group", "query", "memory"), None),
            P(("group", "memory"), "query"),
            P(("group", "memory"), "query"),
        ),
        check_vma=False,
    )
```

```python
import functools
import math

import jax
import jax.numpy as jnp
from jax import lax
from jax.experimental import pallas as pl
from jax.experimental.pallas import tpu as pltpu
from jax.sharding import PartitionSpec as P

HEAD_DIM = 128
BLOCK = 128


def joined(value, axis, combine):
    everything = jax.tree.map(lambda part: lax.all_gather(part, axis), value)
    leading = jax.tree.map(lambda part: part[0], everything)

    def hop(k, so_far):
        return combine(so_far, jax.tree.map(lambda part: part[k], everything))

    return lax.fori_loop(1, lax.axis_size(axis), hop, leading)


def combine_stats(first, second):
    top_value = jnp.maximum(first[0], second[0])
    first_factor = jnp.exp(first[0] - top_value)
    second_factor = jnp.exp(second[0] - top_value)
    return (
        top_value,
        first[1] * first_factor + second[1] * second_factor,
        first[2] * first_factor + second[2] * second_factor,
    )


def local_grads(query_rows, grad_rows, key_rows, value_rows, head_blocks, shard_index):
    row_count = query_rows.shape[0]
    query_blocks = row_count // BLOCK
    local_heads = query_rows.shape[1] // HEAD_DIM
    memory_blocks = key_rows.shape[0] // BLOCK
    slot_count = head_blocks.shape[2]
    group_size = math.gcd(query_blocks, 8)
    group_count = query_blocks // group_size
    scale = 1.0 / math.sqrt(HEAD_DIM)

    def split_queries(array):
        return array.reshape(group_count, group_size, BLOCK, local_heads, HEAD_DIM).transpose(
            3, 0, 1, 2, 4
        )

    def split_memory(array):
        return array.reshape(memory_blocks, BLOCK, local_heads, HEAD_DIM).transpose(2, 0, 1, 3)

    query_split = split_queries(query_rows)
    grad_split = split_queries(grad_rows)
    key_split = split_memory(key_rows)
    value_split = split_memory(value_rows)
    local_ids = head_blocks - shard_index * memory_blocks
    live_slots = ((local_ids >= 0) & (local_ids < memory_blocks)).reshape(
        local_heads, group_count, group_size, slot_count
    )
    slot_picks = jnp.clip(local_ids, 0, memory_blocks - 1).reshape(
        local_heads, group_count, group_size, slot_count
    )

    def block_scores(query_group, grad_group, key_head, value_head, picks):
        key_blocks = key_head[picks]
        value_blocks = value_head[picks]
        scores = (
            jnp.einsum(
                "gbd,gskd->gbsk", query_group, key_blocks, preferred_element_type=jnp.float32
            )
            * scale
        )
        prod_grad = jnp.einsum(
            "gbd,gskd->gbsk", grad_group, value_blocks, preferred_element_type=jnp.float32
        )
        return (scores, prod_grad, key_blocks)

    def stats_head(head_inputs):
        query_head, grad_head, key_head, value_head, pick_head, live_head = head_inputs

        def stats_group(group_inputs):
            query_group, grad_group, picks, live_group = group_inputs
            scores, prod_grad, unused_keys = block_scores(
                query_group, grad_group, key_head, value_head, picks
            )
            live_mask = live_group[:, None, :, None]
            top_value = jnp.max(jnp.where(live_mask, scores, -1e30), axis=(2, 3))
            weight = jnp.where(live_mask, jnp.exp(scores - top_value[:, :, None, None]), 0.0)
            return (
                top_value,
                jnp.sum(weight, axis=(2, 3)),
                jnp.sum(weight * prod_grad, axis=(2, 3)),
            )

        return lax.map(stats_group, (query_head, grad_head, pick_head, live_head))

    top_value, total, weighted = lax.map(
        stats_head, (query_split, grad_split, key_split, value_split, slot_picks, live_slots)
    )
    top_value, total, weighted = joined((top_value, total, weighted), "memory", combine_stats)
    log_total = top_value + jnp.log(total)
    delta_row = weighted / total

    def grads_head(head_inputs):
        query_head, grad_head, key_head, value_head, pick_head, live_head, log_head, delta_head = (
            head_inputs
        )

        def grads_group(carry, group_inputs):
            query_group, grad_group, picks, live_group, log_group, delta_group = group_inputs
            scores, prod_grad, key_blocks = block_scores(
                query_group, grad_group, key_head, value_head, picks
            )
            live_mask = live_group[:, None, :, None]
            probs = jnp.where(live_mask, jnp.exp(scores - log_group[:, :, None, None]), 0.0)
            probs_half = probs.astype(jnp.bfloat16)
            score_grad = (probs * (prod_grad - delta_group[:, :, None, None])).astype(jnp.bfloat16)
            value_terms = jnp.einsum(
                "gbsk,gbd->gskd", probs_half, grad_group, preferred_element_type=jnp.float32
            )
            key_terms = (
                jnp.einsum(
                    "gbsk,gbd->gskd", score_grad, query_group, preferred_element_type=jnp.float32
                )
                * scale
            )
            query_terms = (
                jnp.einsum(
                    "gbsk,gskd->gbd", score_grad, key_blocks, preferred_element_type=jnp.float32
                )
                * scale
            )
            flat_picks = picks.reshape(-1)
            flat_live = live_group.reshape(-1)[:, None, None]
            key_total = (
                carry[0]
                .at[flat_picks]
                .add(jnp.where(flat_live, key_terms.reshape(-1, BLOCK, HEAD_DIM), 0.0))
            )
            value_total = (
                carry[1]
                .at[flat_picks]
                .add(jnp.where(flat_live, value_terms.reshape(-1, BLOCK, HEAD_DIM), 0.0))
            )
            return ((key_total, value_total), query_terms)

        zero_grad = jnp.zeros((memory_blocks, BLOCK, HEAD_DIM), jnp.float32)
        totals, query_terms = lax.scan(
            grads_group,
            (zero_grad, zero_grad),
            (query_head, grad_head, pick_head, live_head, log_head, delta_head),
        )
        return (query_terms, totals[0], totals[1])

    query_grad, key_grad, value_grad = lax.map(
        grads_head,
        (
            query_split,
            grad_split,
            key_split,
            value_split,
            slot_picks,
            live_slots,
            log_total,
            delta_row,
        ),
    )
    query_grad = query_grad.transpose(1, 2, 3, 0, 4).reshape(row_count, local_heads * HEAD_DIM)
    key_grad = key_grad.transpose(1, 2, 0, 3).reshape(memory_blocks * BLOCK, local_heads * HEAD_DIM)
    value_grad = value_grad.transpose(1, 2, 0, 3).reshape(
        memory_blocks * BLOCK, local_heads * HEAD_DIM
    )
    return (query_grad, key_grad, value_grad)


def span_shards(queries, keys, values, grad_out, blocks):
    query_span, grad_span = (
        lax.all_gather(queries, "memory", axis=0, tiled=True),
        lax.all_gather(grad_out, "memory", axis=0, tiled=True),
    )
    query_index = lax.axis_index("query")
    memory_index = lax.axis_index("memory")
    key_rows, value_rows = (
        lax.all_gather(keys, "query", axis=1, tiled=True),
        lax.all_gather(values, "query", axis=1, tiled=True),
    )
    span_blocks = query_span.shape[0] // BLOCK
    head_blocks = lax.dynamic_slice_in_dim(blocks, query_index * span_blocks, span_blocks, 1)
    query_part, key_full, value_full = local_grads(
        query_span, grad_span, key_rows, value_rows, head_blocks, memory_index
    )
    key_grad, value_grad = (
        lax.psum_scatter(key_full, "query", scatter_dimension=1, tiled=True),
        lax.psum_scatter(value_full, "query", scatter_dimension=1, tiled=True),
    )
    grad_query = lax.psum_scatter(
        query_part.astype(jnp.bfloat16), "memory", scatter_dimension=0, tiled=True
    )
    return (grad_query, key_grad.astype(jnp.bfloat16), value_grad.astype(jnp.bfloat16))


MESH = pl.DeviceIdType.MESH
NT = (((1,), (1,)), ((), ()))
TN = (((0,), (0,)), ((), ()))
UNROLL = 2


def position():
    memory_size = lax.axis_size("memory")
    here = lax.axis_index("query") * memory_size + lax.axis_index("memory")
    return lax.axis_index("group"), here, memory_size


def meet(group, here, devices, memory_size):
    barrier = pltpu.get_barrier_semaphore()
    for step in range(1, devices):
        peer = lax.rem(here + step, devices)
        pl.semaphore_signal(
            barrier,
            inc=1,
            device_id=(group, peer // memory_size, lax.rem(peer, memory_size)),
            device_id_type=MESH,
        )
    pl.semaphore_wait(barrier, devices - 1)


def columns(index, width):
    return pl.ds(pl.multiple_of(index * width, width), width)


def rows(index, size):
    return pl.ds(pl.multiple_of(index * size, size), size)


def away(group, memory_size, peer):
    return (group, peer // memory_size, lax.rem(peer, memory_size))


def fused_kernel(
    devices, half, heads,
    picks, earlier, latest, live_ref, query_ref, grad_ref, key_ref, value_ref,
    query_out, key_out, value_out,
    query_in, grad_in, key_in, value_in, weights, products, stats, other, key_sums, value_sums,
    query_stage, key_stage, value_stage, parts,
    in_send, in_recv, in_own, stat_send, stat_recv, out_send, out_recv, out_own,
):
    scale = 1.0 / math.sqrt(HEAD_DIM)
    group, here, memory_size = position()
    my_query, my_memory = here // memory_size, lax.rem(here, memory_size)
    side, lane = my_memory // half, lax.rem(my_memory, half)
    partner = (group, my_query, lax.rem(my_memory + half, memory_size))
    row_count, own_blocks = query_ref.shape[0], key_ref.shape[0]
    memory_rows = own_blocks * BLOCK
    query_blocks = query_in.shape[1] // BLOCK
    half_blocks = key_in[0].shape[0]
    slots = 2 * query_blocks
    meet(group, here, devices, memory_size)

    def transfer(source, target, step, device, send, recv, own):
        if step == 0:
            return pltpu.make_async_copy(source, target, own)
        return pltpu.make_async_remote_copy(
            src_ref=source, dst_ref=target, send_sem=send, recv_sem=recv,
            device_id=device, device_id_type=MESH,
        )

    arrivals = []
    for head in range(heads):
        copies = []
        for which, (source, target) in enumerate(((key_ref, key_in), (value_ref, value_in))):
            for step in range(half):
                peer = lax.rem(lane + step, half)
                at = 2 * devices + which * half + step
                copies.append(transfer(
                    source.at[:, :, columns(peer * heads + head, HEAD_DIM)],
                    target[head].at[pl.ds(lane * own_blocks, own_blocks)],
                    step, (group, my_query, side * half + peer),
                    in_send.at[head, at], in_recv.at[head, at], in_own.at[head, which],
                ))
        for step in range(devices):
            peer = lax.rem(here + step, devices)
            first = (peer // memory_size * half + lax.rem(lax.rem(peer, memory_size), half)) * heads
            for which, (source, target) in enumerate(((query_ref, query_in), (grad_ref, grad_in))):
                at = which * devices + step
                copies.append(transfer(
                    source.at[:, columns(first + head, HEAD_DIM)],
                    target.at[head, rows(here, row_count), :],
                    step, away(group, memory_size, peer),
                    in_send.at[head, at], in_recv.at[head, at], in_own.at[head, 2 + which],
                ))
        for copy in copies:
            copy.start()
        arrivals.append(copies)

    key_sums[0] = jnp.zeros(key_sums.shape[1:], jnp.float32)
    value_sums[0] = jnp.zeros(value_sums.shape[1:], jnp.float32)
    returns, pending = [], []
    for head in range(heads):
        for copy in arrivals[head]:
            copy.wait()
        for copy in pending:
            copy.start()

        def pick(block, slot):
            number = head * slots + 2 * block + slot
            return picks[number], live_ref[pl.ds(number, 1), :]

        def stats_step(block, carry):
            mine = rows(block, BLOCK)
            query, grad = query_in[head, mine, :], grad_in[head, mine, :]
            scores = []
            for slot in range(2):
                place, live = pick(block, slot)
                score = lax.dot_general(
                    key_in[head][place], query, NT, preferred_element_type=jnp.float32
                )
                scores.append(jnp.where(live > 0.0, score * scale, -1e30))
                products[2 * block + slot] = lax.dot_general(
                    value_in[head][place], grad, NT, preferred_element_type=jnp.float32
                )
            top = jnp.maximum(
                jnp.max(scores[0], axis=0, keepdims=True), jnp.max(scores[1], axis=0, keepdims=True)
            )
            total, weighted = 0.0, 0.0
            for slot in range(2):
                place, live = pick(block, slot)
                weight = jnp.exp(scores[slot] - top) * live
                weights[2 * block + slot] = weight
                total += jnp.sum(weight, axis=0, keepdims=True)
                weighted += jnp.sum(weight * products[2 * block + slot], axis=0, keepdims=True)
            line = pl.ds(block, 1)
            stats[head, 0, line, :] = top
            stats[head, 1, line, :] = total
            stats[head, 2, line, :] = weighted
            return carry

        lax.fori_loop(0, query_blocks, stats_step, 0, unroll=UNROLL)
        exchange = pltpu.make_async_remote_copy(
            src_ref=stats.at[head], dst_ref=other.at[head],
            send_sem=stat_send.at[head], recv_sem=stat_recv.at[head],
            device_id=partner, device_id_type=MESH,
        )
        exchange.start()
        exchange.wait()
        ours = (stats[head, 0], stats[head, 1], stats[head, 2])
        top, total, weighted = combine_stats(ours, (other[head, 0], other[head, 1], other[head, 2]))
        stats[head, 0] = jnp.exp(ours[0] - top) / total
        stats[head, 1] = weighted / total

        def grads_step(block, carry):
            mine, line = rows(block, BLOCK), pl.ds(block, 1)
            query, grad = query_in[head, mine, :], grad_in[head, mine, :]
            factor, delta = stats[head, 0, line, :], stats[head, 1, line, :]
            query_term = 0.0
            plain = (((1,), (0,)), ((), ()))
            key_terms, value_terms = [], []
            for slot in range(2):
                place, live = pick(block, slot)
                number = 2 * block + slot
                probs = weights[number] * factor
                score_grad = (probs * (products[number] - delta)).astype(jnp.bfloat16)
                value_terms.append(lax.dot_general(
                    probs.astype(jnp.bfloat16), grad, plain, preferred_element_type=jnp.float32
                ))
                key_terms.append(lax.dot_general(
                    score_grad, query, plain, preferred_element_type=jnp.float32
                ))
                query_term += lax.dot_general(
                    score_grad, key_in[head][place], TN, preferred_element_type=jnp.float32
                )
            query_stage[head, mine, :] = (query_term * scale).astype(query_stage.dtype)
            for slot in range(2):
                number = 2 * block + slot
                before = earlier[head * slots + number]
                key_sums[number + 1] = key_sums[before] + key_terms[slot]
                value_sums[number + 1] = value_sums[before] + value_terms[slot]
            return carry

        lax.fori_loop(0, query_blocks, grads_step, 0, unroll=UNROLL)

        def finish_step(block, carry):
            last = latest[head * half_blocks + block]
            mine = rows(block, BLOCK)
            key_stage[head, mine, :] = (key_sums[last] * scale).astype(key_stage.dtype)
            value_stage[head, mine, :] = value_sums[last].astype(value_stage.dtype)
            return carry

        lax.fori_loop(0, half_blocks, finish_step, 0, unroll=UNROLL)

        copies = []
        for which, (source, target) in enumerate(((key_stage, key_out), (value_stage, value_out))):
            for step in range(half):
                peer = lax.rem(lane + step, half)
                at = devices + which * half + step
                copies.append(transfer(
                    source.at[head, rows(peer, memory_rows), :],
                    target.at[:, columns(lane * heads + head, HEAD_DIM)],
                    step, (group, my_query, side * half + peer),
                    out_send.at[head, at], out_recv.at[head, at], out_own.at[head, which],
                ))
        for step in range(devices):
            peer = lax.rem(here + step, devices)
            copies.append(transfer(
                query_stage.at[head, rows(peer, row_count), :],
                parts.at[side, :, columns((my_query * half + lane) * heads + head, HEAD_DIM)],
                step, away(group, memory_size, peer),
                out_send.at[head, step], out_recv.at[head, step], out_own.at[head, 2],
            ))
        returns += copies
        pending = copies

    for copy in pending:
        copy.start()
    for copy in returns:
        copy.wait()
    query_out[...] = (parts[0].astype(jnp.float32) + parts[1].astype(jnp.float32)).astype(
        query_out.dtype
    )


def head_shards(queries, keys, values, grad_out, blocks):
    memory_size = lax.axis_size("memory")
    devices = lax.axis_size("query") * memory_size
    half = memory_size // 2
    row_count, memory_rows = queries.shape[0], keys.shape[0]
    all_rows, half_rows = row_count * devices, memory_rows * half
    heads = keys.shape[1] // half // HEAD_DIM
    query_blocks, half_blocks = all_rows // BLOCK, half_rows // BLOCK
    slots = 2 * query_blocks
    anywhere, vmem = pl.BlockSpec(memory_space=pl.ANY), pl.BlockSpec(memory_space=pltpu.VMEM)
    smem = pl.BlockSpec(memory_space=pltpu.SMEM)

    my_query, my_memory = lax.axis_index("query"), lax.axis_index("memory")
    first_head = (my_query * half + my_memory % half) * heads
    picks = lax.dynamic_slice_in_dim(blocks, first_head, heads, 0).reshape(heads, slots)
    picks = picks - my_memory // half * half_blocks
    inside = (picks >= 0) & (picks < half_blocks)
    live = jnp.broadcast_to(inside.reshape(-1, 1), (heads * slots, BLOCK)).astype(jnp.float32)
    numbers = jnp.arange(slots, dtype=jnp.int32)
    same = (picks[:, :, None] == picks[:, None, :]) & (numbers[:, None] > numbers[None, :])
    earlier = jnp.max(jnp.where(same, numbers + 1, 0), axis=2)
    named = picks[:, None, :] == jnp.arange(half_blocks, dtype=jnp.int32)[:, None]
    latest = jnp.max(jnp.where(named, numbers + 1, 0), axis=2)

    places = jnp.clip(picks, 0, half_blocks - 1)

    def blocked(array):
        return array.reshape(-1, BLOCK, array.shape[1])

    def half_precision(*shape):
        return pltpu.VMEM(shape, jnp.bfloat16)

    def single_precision(*shape):
        return pltpu.VMEM(shape, jnp.float32)

    def semaphores(*shape):
        return pltpu.SemaphoreType.DMA(shape)

    arrivals, returns = 2 * devices + 2 * half, devices + 2 * half
    return pl.pallas_call(
        functools.partial(fused_kernel, devices, half, heads),
        out_shape=(
            jax.ShapeDtypeStruct(queries.shape, jnp.bfloat16),
            jax.ShapeDtypeStruct(keys.shape, jnp.bfloat16),
            jax.ShapeDtypeStruct(values.shape, jnp.bfloat16),
        ),
        in_specs=[smem] * 3 + [vmem] + [anywhere] * 4,
        out_specs=(vmem, anywhere, anywhere),
        scratch_shapes=[
            half_precision(heads, all_rows, HEAD_DIM),
            half_precision(heads, all_rows, HEAD_DIM),
            [half_precision(half_blocks, BLOCK, HEAD_DIM)] * heads,
            [half_precision(half_blocks, BLOCK, HEAD_DIM)] * heads,
            single_precision(slots, BLOCK, BLOCK),
            single_precision(slots, BLOCK, BLOCK),
            single_precision(heads, 3, query_blocks, BLOCK),
            single_precision(heads, 3, query_blocks, BLOCK),
            single_precision(slots + 1, BLOCK, HEAD_DIM),
            single_precision(slots + 1, BLOCK, HEAD_DIM),
            half_precision(heads, all_rows, HEAD_DIM),
            half_precision(heads, half_rows, HEAD_DIM),
            half_precision(heads, half_rows, HEAD_DIM),
            half_precision(2, row_count, queries.shape[1]),
            semaphores(heads, arrivals),
            semaphores(heads, arrivals),
            semaphores(heads, 4),
            semaphores(heads),
            semaphores(heads),
            semaphores(heads, returns),
            semaphores(heads, returns),
            semaphores(heads, 3),
        ],
        compiler_params=pltpu.CompilerParams(
            collective_id=0, has_side_effects=True, vmem_limit_bytes=62 * 1024 * 1024
        ),
        name="head_grads",
    )(
        places.reshape(-1), earlier.reshape(-1), latest.reshape(-1),
        live, queries, grad_out, blocked(keys), blocked(values),
    )


def shards(queries, keys, values, grad_out, blocks):
    memory_size = lax.axis_size("memory")
    whole_heads = keys.shape[1] % (memory_size // 2 * HEAD_DIM) == 0
    if memory_size % 2 == 0 and whole_heads and blocks.shape[2] == 2:
        return head_shards(queries, keys, values, grad_out, blocks)
    return span_shards(queries, keys, values, grad_out, blocks)


def solution(mesh):
    placed = (
        P(("group", "query", "memory"), None),
        P(("group", "memory"), "query"),
        P(("group", "memory"), "query"),
        P(("group", "query", "memory"), None),
        P(None, "group", None),
    )
    return jax.shard_map(
        shards,
        mesh=mesh,
        in_specs=placed,
        out_specs=(
            P(("group", "query", "memory"), None),
            P(("group", "memory"), "query"),
            P(("group", "memory"), "query"),
        ),
        check_vma=False,
    )
```

```python
import functools
import math

import jax
import jax.numpy as jnp
from jax import lax
from jax.experimental import pallas as pl
from jax.experimental.pallas import tpu as pltpu
from jax.sharding import PartitionSpec as P

HEAD_DIM = 128
BLOCK = 128


def joined(value, axis, combine):
    everything = jax.tree.map(lambda part: lax.all_gather(part, axis), value)
    leading = jax.tree.map(lambda part: part[0], everything)

    def hop(k, so_far):
        return combine(so_far, jax.tree.map(lambda part: part[k], everything))

    return lax.fori_loop(1, lax.axis_size(axis), hop, leading)


def combine_stats(first, second):
    top_value = jnp.maximum(first[0], second[0])
    first_factor = jnp.exp(first[0] - top_value)
    second_factor = jnp.exp(second[0] - top_value)
    return (
        top_value,
        first[1] * first_factor + second[1] * second_factor,
        first[2] * first_factor + second[2] * second_factor,
    )


def local_grads(query_rows, grad_rows, key_rows, value_rows, head_blocks, shard_index):
    row_count = query_rows.shape[0]
    query_blocks = row_count // BLOCK
    local_heads = query_rows.shape[1] // HEAD_DIM
    memory_blocks = key_rows.shape[0] // BLOCK
    slot_count = head_blocks.shape[2]
    group_size = math.gcd(query_blocks, 8)
    group_count = query_blocks // group_size
    scale = 1.0 / math.sqrt(HEAD_DIM)

    def split_queries(array):
        return array.reshape(group_count, group_size, BLOCK, local_heads, HEAD_DIM).transpose(
            3, 0, 1, 2, 4
        )

    def split_memory(array):
        return array.reshape(memory_blocks, BLOCK, local_heads, HEAD_DIM).transpose(2, 0, 1, 3)

    query_split = split_queries(query_rows)
    grad_split = split_queries(grad_rows)
    key_split = split_memory(key_rows)
    value_split = split_memory(value_rows)
    local_ids = head_blocks - shard_index * memory_blocks
    live_slots = ((local_ids >= 0) & (local_ids < memory_blocks)).reshape(
        local_heads, group_count, group_size, slot_count
    )
    slot_picks = jnp.clip(local_ids, 0, memory_blocks - 1).reshape(
        local_heads, group_count, group_size, slot_count
    )

    def block_scores(query_group, grad_group, key_head, value_head, picks):
        key_blocks = key_head[picks]
        value_blocks = value_head[picks]
        scores = (
            jnp.einsum(
                "gbd,gskd->gbsk", query_group, key_blocks, preferred_element_type=jnp.float32
            )
            * scale
        )
        prod_grad = jnp.einsum(
            "gbd,gskd->gbsk", grad_group, value_blocks, preferred_element_type=jnp.float32
        )
        return (scores, prod_grad, key_blocks)

    def stats_head(head_inputs):
        query_head, grad_head, key_head, value_head, pick_head, live_head = head_inputs

        def stats_group(group_inputs):
            query_group, grad_group, picks, live_group = group_inputs
            scores, prod_grad, unused_keys = block_scores(
                query_group, grad_group, key_head, value_head, picks
            )
            live_mask = live_group[:, None, :, None]
            top_value = jnp.max(jnp.where(live_mask, scores, -1e30), axis=(2, 3))
            weight = jnp.where(live_mask, jnp.exp(scores - top_value[:, :, None, None]), 0.0)
            return (
                top_value,
                jnp.sum(weight, axis=(2, 3)),
                jnp.sum(weight * prod_grad, axis=(2, 3)),
            )

        return lax.map(stats_group, (query_head, grad_head, pick_head, live_head))

    top_value, total, weighted = lax.map(
        stats_head, (query_split, grad_split, key_split, value_split, slot_picks, live_slots)
    )
    top_value, total, weighted = joined((top_value, total, weighted), "memory", combine_stats)
    log_total = top_value + jnp.log(total)
    delta_row = weighted / total

    def grads_head(head_inputs):
        query_head, grad_head, key_head, value_head, pick_head, live_head, log_head, delta_head = (
            head_inputs
        )

        def grads_group(carry, group_inputs):
            query_group, grad_group, picks, live_group, log_group, delta_group = group_inputs
            scores, prod_grad, key_blocks = block_scores(
                query_group, grad_group, key_head, value_head, picks
            )
            live_mask = live_group[:, None, :, None]
            probs = jnp.where(live_mask, jnp.exp(scores - log_group[:, :, None, None]), 0.0)
            probs_half = probs.astype(jnp.bfloat16)
            score_grad = (probs * (prod_grad - delta_group[:, :, None, None])).astype(jnp.bfloat16)
            value_terms = jnp.einsum(
                "gbsk,gbd->gskd", probs_half, grad_group, preferred_element_type=jnp.float32
            )
            key_terms = (
                jnp.einsum(
                    "gbsk,gbd->gskd", score_grad, query_group, preferred_element_type=jnp.float32
                )
                * scale
            )
            query_terms = (
                jnp.einsum(
                    "gbsk,gskd->gbd", score_grad, key_blocks, preferred_element_type=jnp.float32
                )
                * scale
            )
            flat_picks = picks.reshape(-1)
            flat_live = live_group.reshape(-1)[:, None, None]
            key_total = (
                carry[0]
                .at[flat_picks]
                .add(jnp.where(flat_live, key_terms.reshape(-1, BLOCK, HEAD_DIM), 0.0))
            )
            value_total = (
                carry[1]
                .at[flat_picks]
                .add(jnp.where(flat_live, value_terms.reshape(-1, BLOCK, HEAD_DIM), 0.0))
            )
            return ((key_total, value_total), query_terms)

        zero_grad = jnp.zeros((memory_blocks, BLOCK, HEAD_DIM), jnp.float32)
        totals, query_terms = lax.scan(
            grads_group,
            (zero_grad, zero_grad),
            (query_head, grad_head, pick_head, live_head, log_head, delta_head),
        )
        return (query_terms, totals[0], totals[1])

    query_grad, key_grad, value_grad = lax.map(
        grads_head,
        (
            query_split,
            grad_split,
            key_split,
            value_split,
            slot_picks,
            live_slots,
            log_total,
            delta_row,
        ),
    )
    query_grad = query_grad.transpose(1, 2, 3, 0, 4).reshape(row_count, local_heads * HEAD_DIM)
    key_grad = key_grad.transpose(1, 2, 0, 3).reshape(memory_blocks * BLOCK, local_heads * HEAD_DIM)
    value_grad = value_grad.transpose(1, 2, 0, 3).reshape(
        memory_blocks * BLOCK, local_heads * HEAD_DIM
    )
    return (query_grad, key_grad, value_grad)


def span_shards(queries, keys, values, grad_out, blocks):
    query_span, grad_span = (
        lax.all_gather(queries, "memory", axis=0, tiled=True),
        lax.all_gather(grad_out, "memory", axis=0, tiled=True),
    )
    query_index = lax.axis_index("query")
    memory_index = lax.axis_index("memory")
    key_rows, value_rows = (
        lax.all_gather(keys, "query", axis=1, tiled=True),
        lax.all_gather(values, "query", axis=1, tiled=True),
    )
    span_blocks = query_span.shape[0] // BLOCK
    head_blocks = lax.dynamic_slice_in_dim(blocks, query_index * span_blocks, span_blocks, 1)
    query_part, key_full, value_full = local_grads(
        query_span, grad_span, key_rows, value_rows, head_blocks, memory_index
    )
    key_grad, value_grad = (
        lax.psum_scatter(key_full, "query", scatter_dimension=1, tiled=True),
        lax.psum_scatter(value_full, "query", scatter_dimension=1, tiled=True),
    )
    grad_query = lax.psum_scatter(
        query_part.astype(jnp.bfloat16), "memory", scatter_dimension=0, tiled=True
    )
    return (grad_query, key_grad.astype(jnp.bfloat16), value_grad.astype(jnp.bfloat16))


MESH = pl.DeviceIdType.MESH
NT = (((1,), (1,)), ((), ()))
TN = (((0,), (0,)), ((), ()))
UNROLL = 2


def position():
    memory_size = lax.axis_size("memory")
    here = lax.axis_index("query") * memory_size + lax.axis_index("memory")
    return lax.axis_index("group"), here, memory_size


def meet(group, here, devices, memory_size):
    barrier = pltpu.get_barrier_semaphore()
    for step in range(1, devices):
        peer = lax.rem(here + step, devices)
        pl.semaphore_signal(
            barrier,
            inc=1,
            device_id=(group, peer // memory_size, lax.rem(peer, memory_size)),
            device_id_type=MESH,
        )
    pl.semaphore_wait(barrier, devices - 1)


def columns(index, width):
    return pl.ds(pl.multiple_of(index * width, width), width)


def rows(index, size):
    return pl.ds(pl.multiple_of(index * size, size), size)


def away(group, memory_size, peer):
    return (group, peer // memory_size, lax.rem(peer, memory_size))


def fused_kernel(
    devices, half, heads,
    table, query_ref, grad_ref, key_ref, value_ref,
    parts, key_out, value_out,
    query_in, grad_in, key_in, value_in, weights, products, stats, other, key_sums, value_sums,
    query_stage, key_stage, value_stage,
    in_send, in_recv, in_own, stat_send, stat_recv, out_send, out_recv, out_own,
):
    scale = 1.0 / math.sqrt(HEAD_DIM)
    group, here, memory_size = position()
    my_query, my_memory = here // memory_size, lax.rem(here, memory_size)
    side, lane = my_memory // half, lax.rem(my_memory, half)
    partner = (group, my_query, lax.rem(my_memory + half, memory_size))
    row_count, own_blocks = query_ref.shape[0], key_ref.shape[0]
    memory_rows = own_blocks * BLOCK
    query_blocks = query_in.shape[1] // BLOCK
    half_blocks = key_in[0].shape[0]
    slots = 2 * query_blocks
    lines = 2 * slots + half_blocks
    meet(group, here, devices, memory_size)

    def transfer(source, target, step, device, send, recv, own):
        if step == 0:
            return pltpu.make_async_copy(source, target, own)
        return pltpu.make_async_remote_copy(
            src_ref=source, dst_ref=target, send_sem=send, recv_sem=recv,
            device_id=device, device_id_type=MESH,
        )

    arrivals = []
    for head in range(heads):
        copies = []
        for which, (source, target) in enumerate(((key_ref, key_in), (value_ref, value_in))):
            for step in range(half):
                peer = lax.rem(lane + step, half)
                at = 2 * devices + which * half + step
                copies.append(transfer(
                    source.at[:, :, columns(peer * heads + head, HEAD_DIM)],
                    target[head].at[pl.ds(lane * own_blocks, own_blocks)],
                    step, (group, my_query, side * half + peer),
                    in_send.at[head, at], in_recv.at[head, at], in_own.at[head, which],
                ))
        for step in range(devices):
            peer = lax.rem(here + step, devices)
            first = (peer // memory_size * half + lax.rem(lax.rem(peer, memory_size), half)) * heads
            for which, (source, target) in enumerate(((query_ref, query_in), (grad_ref, grad_in))):
                at = which * devices + step
                copies.append(transfer(
                    source.at[:, columns(first + head, HEAD_DIM)],
                    target.at[head, rows(here, row_count), :],
                    step, away(group, memory_size, peer),
                    in_send.at[head, at], in_recv.at[head, at], in_own.at[head, 2 + which],
                ))
        for copy in copies:
            copy.start()
        arrivals.append(copies)

    key_sums[0] = jnp.zeros(key_sums.shape[1:], jnp.float32)
    value_sums[0] = jnp.zeros(value_sums.shape[1:], jnp.float32)
    returns = []
    for head in range(heads):
        for copy in arrivals[head]:
            copy.wait()

        def pick(block, slot):
            coded = table[head * lines + slots + half_blocks + 2 * block + slot]
            return jnp.maximum(coded - 1, 0), jnp.minimum(coded, 1).astype(jnp.float32)

        def stats_step(block, carry):
            mine = rows(block, BLOCK)
            query, grad = query_in[head, mine, :], grad_in[head, mine, :]
            scores = []
            for slot in range(2):
                place, live = pick(block, slot)
                score = lax.dot_general(
                    key_in[head][place], query, NT, preferred_element_type=jnp.float32
                )
                scores.append(score * (scale * live) + (live - 1.0) * 1e30)
                products[2 * block + slot] = lax.dot_general(
                    value_in[head][place], grad, NT, preferred_element_type=jnp.float32
                )
            top = jnp.maximum(
                jnp.max(scores[0], axis=0, keepdims=True), jnp.max(scores[1], axis=0, keepdims=True)
            )
            total, weighted = 0.0, 0.0
            for slot in range(2):
                place, live = pick(block, slot)
                weight = jnp.exp(scores[slot] - top) * live
                weights[2 * block + slot] = weight
                total += jnp.sum(weight, axis=0, keepdims=True)
                weighted += jnp.sum(weight * products[2 * block + slot], axis=0, keepdims=True)
            line = pl.ds(block, 1)
            stats[head, 0, line, :] = top
            stats[head, 1, line, :] = total
            stats[head, 2, line, :] = weighted
            return carry

        lax.fori_loop(0, query_blocks, stats_step, 0, unroll=UNROLL)
        exchange = pltpu.make_async_remote_copy(
            src_ref=stats.at[head], dst_ref=other.at[head],
            send_sem=stat_send.at[head], recv_sem=stat_recv.at[head],
            device_id=partner, device_id_type=MESH,
        )
        exchange.start()
        exchange.wait()
        ours = (stats[head, 0], stats[head, 1], stats[head, 2])
        top, total, weighted = combine_stats(ours, (other[head, 0], other[head, 1], other[head, 2]))
        stats[head, 0] = jnp.exp(ours[0] - top) / total
        stats[head, 1] = weighted / total

        def grads_step(block, carry):
            mine, line = rows(block, BLOCK), pl.ds(block, 1)
            query, grad = query_in[head, mine, :], grad_in[head, mine, :]
            factor, delta = stats[head, 0, line, :], stats[head, 1, line, :]
            query_term = 0.0
            plain = (((1,), (0,)), ((), ()))
            key_terms, value_terms = [], []
            for slot in range(2):
                place, live = pick(block, slot)
                number = 2 * block + slot
                probs = weights[number] * factor
                score_grad = (probs * (products[number] - delta)).astype(jnp.bfloat16)
                value_terms.append(lax.dot_general(
                    probs.astype(jnp.bfloat16), grad, plain, preferred_element_type=jnp.float32
                ))
                key_terms.append(lax.dot_general(
                    score_grad, query, plain, preferred_element_type=jnp.float32
                ))
                query_term += lax.dot_general(
                    score_grad, key_in[head][place], TN, preferred_element_type=jnp.float32
                )
            query_stage[head, mine, :] = (query_term * scale).astype(query_stage.dtype)
            for slot in range(2):
                number = 2 * block + slot
                before = table[head * lines + number]
                key_sums[number + 1] = key_sums[before] + key_terms[slot]
                value_sums[number + 1] = value_sums[before] + value_terms[slot]
            return carry

        lax.fori_loop(0, query_blocks, grads_step, 0, unroll=UNROLL)

        def finish_step(block, carry):
            last = table[head * lines + slots + block]
            mine = rows(block, BLOCK)
            key_stage[head, mine, :] = (key_sums[last] * scale).astype(key_stage.dtype)
            value_stage[head, mine, :] = value_sums[last].astype(value_stage.dtype)
            return carry

        lax.fori_loop(0, half_blocks, finish_step, 0, unroll=UNROLL)

        copies = []
        for which, (source, target) in enumerate(((key_stage, key_out), (value_stage, value_out))):
            for step in range(half):
                peer = lax.rem(lane + step, half)
                at = devices + which * half + step
                copies.append(transfer(
                    source.at[head, rows(peer, memory_rows), :],
                    target.at[:, columns(lane * heads + head, HEAD_DIM)],
                    step, (group, my_query, side * half + peer),
                    out_send.at[head, at], out_recv.at[head, at], out_own.at[head, which],
                ))
        for step in range(devices):
            peer = lax.rem(here + step, devices)
            copies.append(transfer(
                query_stage.at[head, rows(peer, row_count), :],
                parts.at[side, :, columns((my_query * half + lane) * heads + head, HEAD_DIM)],
                step, away(group, memory_size, peer),
                out_send.at[head, step], out_recv.at[head, step], out_own.at[head, 2],
            ))
        for copy in copies:
            copy.start()
        returns += copies

    for copy in returns:
        copy.wait()


def head_shards(queries, keys, values, grad_out, blocks):
    memory_size = lax.axis_size("memory")
    devices = lax.axis_size("query") * memory_size
    half = memory_size // 2
    row_count, memory_rows = queries.shape[0], keys.shape[0]
    all_rows, half_rows = row_count * devices, memory_rows * half
    heads = keys.shape[1] // half // HEAD_DIM
    query_blocks, half_blocks = all_rows // BLOCK, half_rows // BLOCK
    slots = 2 * query_blocks
    anywhere = pl.BlockSpec(memory_space=pl.ANY)
    smem = pl.BlockSpec(memory_space=pltpu.SMEM)

    my_query, my_memory = lax.axis_index("query"), lax.axis_index("memory")
    first_head = (my_query * half + my_memory % half) * heads
    picks = lax.dynamic_slice_in_dim(blocks, first_head, heads, 0).reshape(heads, slots)
    picks = picks - my_memory // half * half_blocks
    inside = (picks >= 0) & (picks < half_blocks)
    coded = jnp.where(inside, picks + 1, 0)
    line = jnp.arange(2 * slots + half_blocks, dtype=jnp.int32)[:, None]
    number = jnp.arange(slots, dtype=jnp.int32)[None, :]
    ids = jnp.broadcast_to(jnp.arange(half_blocks, dtype=jnp.int32), (heads, half_blocks))
    wanted = jnp.concatenate([picks, ids, picks], axis=1)[:, :, None]
    first_part = line < slots + half_blocks
    chosen = jnp.where(
        first_part,
        (wanted == picks[:, None, :]) & ((line >= slots) | (number < line)),
        line - slots - half_blocks == number,
    )
    table = jnp.max(
        jnp.where(chosen, jnp.where(first_part, number + 1, coded[:, None, :]), 0), axis=2
    ).reshape(-1)

    def blocked(array):
        return array.reshape(-1, BLOCK, array.shape[1])

    def half_precision(*shape):
        return pltpu.VMEM(shape, jnp.bfloat16)

    def single_precision(*shape):
        return pltpu.VMEM(shape, jnp.float32)

    def semaphores(*shape):
        return pltpu.SemaphoreType.DMA(shape)

    arrivals, returns = 2 * devices + 2 * half, devices + 2 * half
    parts, key_grad, value_grad = pl.pallas_call(
        functools.partial(fused_kernel, devices, half, heads),
        out_shape=(
            jax.ShapeDtypeStruct((2, *queries.shape), jnp.bfloat16),
            jax.ShapeDtypeStruct(keys.shape, jnp.bfloat16),
            jax.ShapeDtypeStruct(values.shape, jnp.bfloat16),
        ),
        in_specs=[smem] + [anywhere] * 4,
        out_specs=(anywhere,) * 3,
        scratch_shapes=[
            half_precision(heads, all_rows, HEAD_DIM),
            half_precision(heads, all_rows, HEAD_DIM),
            [half_precision(half_blocks, BLOCK, HEAD_DIM)] * heads,
            [half_precision(half_blocks, BLOCK, HEAD_DIM)] * heads,
            single_precision(slots, BLOCK, BLOCK),
            single_precision(slots, BLOCK, BLOCK),
            single_precision(heads, 3, query_blocks, BLOCK),
            single_precision(heads, 3, query_blocks, BLOCK),
            single_precision(slots + 1, BLOCK, HEAD_DIM),
            single_precision(slots + 1, BLOCK, HEAD_DIM),
            half_precision(heads, all_rows, HEAD_DIM),
            half_precision(heads, half_rows, HEAD_DIM),
            half_precision(heads, half_rows, HEAD_DIM),
            semaphores(heads, arrivals),
            semaphores(heads, arrivals),
            semaphores(heads, 4),
            semaphores(heads),
            semaphores(heads),
            semaphores(heads, returns),
            semaphores(heads, returns),
            semaphores(heads, 3),
        ],
        compiler_params=pltpu.CompilerParams(
            collective_id=0, has_side_effects=True, vmem_limit_bytes=62 * 1024 * 1024
        ),
        name="head_grads",
    )(table, queries, grad_out, blocked(keys), blocked(values))

    query_grad = parts[0].astype(jnp.float32) + parts[1].astype(jnp.float32)
    return (query_grad.astype(jnp.bfloat16), key_grad, value_grad)


def shards(queries, keys, values, grad_out, blocks):
    memory_size = lax.axis_size("memory")
    whole_heads = keys.shape[1] % (memory_size // 2 * HEAD_DIM) == 0
    if memory_size % 2 == 0 and whole_heads and blocks.shape[2] == 2:
        return head_shards(queries, keys, values, grad_out, blocks)
    return span_shards(queries, keys, values, grad_out, blocks)


def solution(mesh):
    placed = (
        P(("group", "query", "memory"), None),
        P(("group", "memory"), "query"),
        P(("group", "memory"), "query"),
        P(("group", "query", "memory"), None),
        P(None, "group", None),
    )
    return jax.shard_map(
        shards,
        mesh=mesh,
        in_specs=placed,
        out_specs=(
            P(("group", "query", "memory"), None),
            P(("group", "memory"), "query"),
            P(("group", "memory"), "query"),
        ),
        check_vma=False,
    )
```

```python
import functools
import math

import jax
import jax.numpy as jnp
from jax import lax
from jax.experimental import pallas as pl
from jax.experimental.pallas import tpu as pltpu
from jax.sharding import PartitionSpec as P

HEAD_DIM = 128
BLOCK = 128


def joined(value, axis, combine):
    everything = jax.tree.map(lambda part: lax.all_gather(part, axis), value)
    leading = jax.tree.map(lambda part: part[0], everything)

    def hop(k, so_far):
        return combine(so_far, jax.tree.map(lambda part: part[k], everything))

    return lax.fori_loop(1, lax.axis_size(axis), hop, leading)


def combine_stats(first, second):
    top_value = jnp.maximum(first[0], second[0])
    first_factor = jnp.exp(first[0] - top_value)
    second_factor = jnp.exp(second[0] - top_value)
    return (
        top_value,
        first[1] * first_factor + second[1] * second_factor,
        first[2] * first_factor + second[2] * second_factor,
    )


def local_grads(query_rows, grad_rows, key_rows, value_rows, head_blocks, shard_index):
    row_count = query_rows.shape[0]
    query_blocks = row_count // BLOCK
    local_heads = query_rows.shape[1] // HEAD_DIM
    memory_blocks = key_rows.shape[0] // BLOCK
    slot_count = head_blocks.shape[2]
    group_size = math.gcd(query_blocks, 8)
    group_count = query_blocks // group_size
    scale = 1.0 / math.sqrt(HEAD_DIM)

    def split_queries(array):
        return array.reshape(group_count, group_size, BLOCK, local_heads, HEAD_DIM).transpose(
            3, 0, 1, 2, 4
        )

    def split_memory(array):
        return array.reshape(memory_blocks, BLOCK, local_heads, HEAD_DIM).transpose(2, 0, 1, 3)

    query_split = split_queries(query_rows)
    grad_split = split_queries(grad_rows)
    key_split = split_memory(key_rows)
    value_split = split_memory(value_rows)
    local_ids = head_blocks - shard_index * memory_blocks
    live_slots = ((local_ids >= 0) & (local_ids < memory_blocks)).reshape(
        local_heads, group_count, group_size, slot_count
    )
    slot_picks = jnp.clip(local_ids, 0, memory_blocks - 1).reshape(
        local_heads, group_count, group_size, slot_count
    )

    def block_scores(query_group, grad_group, key_head, value_head, picks):
        key_blocks = key_head[picks]
        value_blocks = value_head[picks]
        scores = (
            jnp.einsum(
                "gbd,gskd->gbsk", query_group, key_blocks, preferred_element_type=jnp.float32
            )
            * scale
        )
        prod_grad = jnp.einsum(
            "gbd,gskd->gbsk", grad_group, value_blocks, preferred_element_type=jnp.float32
        )
        return (scores, prod_grad, key_blocks)

    def stats_head(head_inputs):
        query_head, grad_head, key_head, value_head, pick_head, live_head = head_inputs

        def stats_group(group_inputs):
            query_group, grad_group, picks, live_group = group_inputs
            scores, prod_grad, unused_keys = block_scores(
                query_group, grad_group, key_head, value_head, picks
            )
            live_mask = live_group[:, None, :, None]
            top_value = jnp.max(jnp.where(live_mask, scores, -1e30), axis=(2, 3))
            weight = jnp.where(live_mask, jnp.exp(scores - top_value[:, :, None, None]), 0.0)
            return (
                top_value,
                jnp.sum(weight, axis=(2, 3)),
                jnp.sum(weight * prod_grad, axis=(2, 3)),
            )

        return lax.map(stats_group, (query_head, grad_head, pick_head, live_head))

    top_value, total, weighted = lax.map(
        stats_head, (query_split, grad_split, key_split, value_split, slot_picks, live_slots)
    )
    top_value, total, weighted = joined((top_value, total, weighted), "memory", combine_stats)
    log_total = top_value + jnp.log(total)
    delta_row = weighted / total

    def grads_head(head_inputs):
        query_head, grad_head, key_head, value_head, pick_head, live_head, log_head, delta_head = (
            head_inputs
        )

        def grads_group(carry, group_inputs):
            query_group, grad_group, picks, live_group, log_group, delta_group = group_inputs
            scores, prod_grad, key_blocks = block_scores(
                query_group, grad_group, key_head, value_head, picks
            )
            live_mask = live_group[:, None, :, None]
            probs = jnp.where(live_mask, jnp.exp(scores - log_group[:, :, None, None]), 0.0)
            probs_half = probs.astype(jnp.bfloat16)
            score_grad = (probs * (prod_grad - delta_group[:, :, None, None])).astype(jnp.bfloat16)
            value_terms = jnp.einsum(
                "gbsk,gbd->gskd", probs_half, grad_group, preferred_element_type=jnp.float32
            )
            key_terms = (
                jnp.einsum(
                    "gbsk,gbd->gskd", score_grad, query_group, preferred_element_type=jnp.float32
                )
                * scale
            )
            query_terms = (
                jnp.einsum(
                    "gbsk,gskd->gbd", score_grad, key_blocks, preferred_element_type=jnp.float32
                )
                * scale
            )
            flat_picks = picks.reshape(-1)
            flat_live = live_group.reshape(-1)[:, None, None]
            key_total = (
                carry[0]
                .at[flat_picks]
                .add(jnp.where(flat_live, key_terms.reshape(-1, BLOCK, HEAD_DIM), 0.0))
            )
            value_total = (
                carry[1]
                .at[flat_picks]
                .add(jnp.where(flat_live, value_terms.reshape(-1, BLOCK, HEAD_DIM), 0.0))
            )
            return ((key_total, value_total), query_terms)

        zero_grad = jnp.zeros((memory_blocks, BLOCK, HEAD_DIM), jnp.float32)
        totals, query_terms = lax.scan(
            grads_group,
            (zero_grad, zero_grad),
            (query_head, grad_head, pick_head, live_head, log_head, delta_head),
        )
        return (query_terms, totals[0], totals[1])

    query_grad, key_grad, value_grad = lax.map(
        grads_head,
        (
            query_split,
            grad_split,
            key_split,
            value_split,
            slot_picks,
            live_slots,
            log_total,
            delta_row,
        ),
    )
    query_grad = query_grad.transpose(1, 2, 3, 0, 4).reshape(row_count, local_heads * HEAD_DIM)
    key_grad = key_grad.transpose(1, 2, 0, 3).reshape(memory_blocks * BLOCK, local_heads * HEAD_DIM)
    value_grad = value_grad.transpose(1, 2, 0, 3).reshape(
        memory_blocks * BLOCK, local_heads * HEAD_DIM
    )
    return (query_grad, key_grad, value_grad)


def span_shards(queries, keys, values, grad_out, blocks):
    query_span, grad_span = (
        lax.all_gather(queries, "memory", axis=0, tiled=True),
        lax.all_gather(grad_out, "memory", axis=0, tiled=True),
    )
    query_index = lax.axis_index("query")
    memory_index = lax.axis_index("memory")
    key_rows, value_rows = (
        lax.all_gather(keys, "query", axis=1, tiled=True),
        lax.all_gather(values, "query", axis=1, tiled=True),
    )
    span_blocks = query_span.shape[0] // BLOCK
    head_blocks = lax.dynamic_slice_in_dim(blocks, query_index * span_blocks, span_blocks, 1)
    query_part, key_full, value_full = local_grads(
        query_span, grad_span, key_rows, value_rows, head_blocks, memory_index
    )
    key_grad, value_grad = (
        lax.psum_scatter(key_full, "query", scatter_dimension=1, tiled=True),
        lax.psum_scatter(value_full, "query", scatter_dimension=1, tiled=True),
    )
    grad_query = lax.psum_scatter(
        query_part.astype(jnp.bfloat16), "memory", scatter_dimension=0, tiled=True
    )
    return (grad_query, key_grad.astype(jnp.bfloat16), value_grad.astype(jnp.bfloat16))


MESH = pl.DeviceIdType.MESH
NT = (((1,), (1,)), ((), ()))
TN = (((0,), (0,)), ((), ()))
UNROLL = 4


def position():
    memory_size = lax.axis_size("memory")
    here = lax.axis_index("query") * memory_size + lax.axis_index("memory")
    return lax.axis_index("group"), here, memory_size


def meet(group, here, devices, memory_size):
    barrier = pltpu.get_barrier_semaphore()
    for step in range(1, devices):
        peer = lax.rem(here + step, devices)
        pl.semaphore_signal(
            barrier,
            inc=1,
            device_id=(group, peer // memory_size, lax.rem(peer, memory_size)),
            device_id_type=MESH,
        )
    pl.semaphore_wait(barrier, devices - 1)


def columns(index, width):
    return pl.ds(pl.multiple_of(index * width, width), width)


def rows(index, size):
    return pl.ds(pl.multiple_of(index * size, size), size)


def away(group, memory_size, peer):
    return (group, peer // memory_size, lax.rem(peer, memory_size))


def fused_kernel(
    devices, half, heads,
    table, query_ref, grad_ref, key_ref, value_ref,
    parts, key_out, value_out,
    query_in, grad_in, key_in, value_in, weights, products, stats, other, key_sums, value_sums,
    query_stage, key_stage, value_stage,
    in_send, in_recv, in_own, stat_send, stat_recv, out_send, out_recv, out_own,
):
    scale = 1.0 / math.sqrt(HEAD_DIM)
    group, here, memory_size = position()
    my_query, my_memory = here // memory_size, lax.rem(here, memory_size)
    side, lane = my_memory // half, lax.rem(my_memory, half)
    partner = (group, my_query, lax.rem(my_memory + half, memory_size))
    row_count, own_blocks = query_ref.shape[0], key_ref.shape[0]
    memory_rows = own_blocks * BLOCK
    query_blocks = query_in.shape[1] // BLOCK
    half_blocks = key_in[0].shape[0]
    slots = 2 * query_blocks
    lines = 2 * slots + half_blocks
    meet(group, here, devices, memory_size)

    query_size = devices // memory_size
    peers = []
    for hop in (*range(memory_size // 2, 0, -1), *range(memory_size // 2 + 1, memory_size), 0):
        for turn in range(query_size):
            peer_query = lax.rem(my_query + turn, query_size)
            peer_memory = lax.rem(my_memory + hop, memory_size)
            peers.append((hop * query_size + turn, peer_query * memory_size + peer_memory))

    def transfer(source, target, step, device, send, recv, own):
        if step == 0:
            return pltpu.make_async_copy(source, target, own)
        return pltpu.make_async_remote_copy(
            src_ref=source, dst_ref=target, send_sem=send, recv_sem=recv,
            device_id=device, device_id_type=MESH,
        )

    arrivals = []
    for head in range(heads):
        copies = []
        for which, (source, target) in enumerate(((key_ref, key_in), (value_ref, value_in))):
            for step in range(half):
                peer = lax.rem(lane + step, half)
                at = 2 * devices + which * half + step
                copies.append(transfer(
                    source.at[:, :, columns(peer * heads + head, HEAD_DIM)],
                    target[head].at[pl.ds(lane * own_blocks, own_blocks)],
                    step, (group, my_query, side * half + peer),
                    in_send.at[head, at], in_recv.at[head, at], in_own.at[head, which],
                ))
        for step, peer in peers:
            first = (peer // memory_size * half + lax.rem(lax.rem(peer, memory_size), half)) * heads
            for which, (source, target) in enumerate(((query_ref, query_in), (grad_ref, grad_in))):
                at = which * devices + step
                copies.append(transfer(
                    source.at[:, columns(first + head, HEAD_DIM)],
                    target.at[head, rows(here, row_count), :],
                    step, away(group, memory_size, peer),
                    in_send.at[head, at], in_recv.at[head, at], in_own.at[head, 2 + which],
                ))
        for copy in copies:
            copy.start()
        arrivals.append(copies)

    key_sums[0] = jnp.zeros(key_sums.shape[1:], jnp.float32)
    value_sums[0] = jnp.zeros(value_sums.shape[1:], jnp.float32)
    returns = []
    for head in range(heads):
        for copy in arrivals[head]:
            copy.wait()

        def pick(block, slot):
            coded = table[head * lines + slots + half_blocks + 2 * block + slot]
            return jnp.maximum(coded - 1, 0), jnp.minimum(coded, 1).astype(jnp.float32)

        def stats_step(block, carry):
            mine = rows(block, BLOCK)
            query, grad = query_in[head, mine, :], grad_in[head, mine, :]
            scores = []
            for slot in range(2):
                place, live = pick(block, slot)
                score = lax.dot_general(
                    key_in[head][place], query, NT, preferred_element_type=jnp.float32
                )
                scores.append(score * (scale * live) + (live - 1.0) * 1e30)
                products[2 * block + slot] = lax.dot_general(
                    value_in[head][place], grad, NT, preferred_element_type=jnp.float32
                )
            top = jnp.maximum(
                jnp.max(scores[0], axis=0, keepdims=True), jnp.max(scores[1], axis=0, keepdims=True)
            )
            total, weighted = 0.0, 0.0
            for slot in range(2):
                place, live = pick(block, slot)
                weight = jnp.exp(scores[slot] - top) * live
                weights[2 * block + slot] = weight
                total += jnp.sum(weight, axis=0, keepdims=True)
                weighted += jnp.sum(weight * products[2 * block + slot], axis=0, keepdims=True)
            line = pl.ds(block, 1)
            stats[head, 0, line, :] = top
            stats[head, 1, line, :] = total
            stats[head, 2, line, :] = weighted
            return carry

        lax.fori_loop(0, query_blocks, stats_step, 0, unroll=UNROLL)
        exchange = pltpu.make_async_remote_copy(
            src_ref=stats.at[head], dst_ref=other.at[head],
            send_sem=stat_send.at[head], recv_sem=stat_recv.at[head],
            device_id=partner, device_id_type=MESH,
        )
        exchange.start()
        exchange.wait()
        ours = (stats[head, 0], stats[head, 1], stats[head, 2])
        top, total, weighted = combine_stats(ours, (other[head, 0], other[head, 1], other[head, 2]))
        stats[head, 0] = jnp.exp(ours[0] - top) / total
        stats[head, 1] = weighted / total

        def grads_step(block, carry):
            mine, line = rows(block, BLOCK), pl.ds(block, 1)
            query, grad = query_in[head, mine, :], grad_in[head, mine, :]
            factor, delta = stats[head, 0, line, :], stats[head, 1, line, :]
            query_term = 0.0
            plain = (((1,), (0,)), ((), ()))
            key_terms, value_terms = [], []
            for slot in range(2):
                place, live = pick(block, slot)
                number = 2 * block + slot
                probs = weights[number] * factor
                score_grad = (probs * (products[number] - delta)).astype(jnp.bfloat16)
                value_terms.append(lax.dot_general(
                    probs.astype(jnp.bfloat16), grad, plain, preferred_element_type=jnp.float32
                ))
                key_terms.append(lax.dot_general(
                    score_grad, query, plain, preferred_element_type=jnp.float32
                ))
                query_term += lax.dot_general(
                    score_grad, key_in[head][place], TN, preferred_element_type=jnp.float32
                )
            query_stage[head, mine, :] = (query_term * scale).astype(query_stage.dtype)
            for slot in range(2):
                number = 2 * block + slot
                before = table[head * lines + number]
                key_sums[number + 1] = key_sums[before] + key_terms[slot]
                value_sums[number + 1] = value_sums[before] + value_terms[slot]
            return carry

        lax.fori_loop(0, query_blocks, grads_step, 0, unroll=UNROLL)

        copies = []
        for step, peer in peers:
            copies.append(transfer(
                query_stage.at[head, rows(peer, row_count), :],
                parts.at[side, :, columns((my_query * half + lane) * heads + head, HEAD_DIM)],
                step, away(group, memory_size, peer),
                out_send.at[head, step], out_recv.at[head, step], out_own.at[head, 2],
            ))
        for copy in copies:
            copy.start()
        returns += copies

        def finish_step(block, carry):
            last = table[head * lines + slots + block]
            mine = rows(block, BLOCK)
            key_stage[head, mine, :] = (key_sums[last] * scale).astype(key_stage.dtype)
            value_stage[head, mine, :] = value_sums[last].astype(value_stage.dtype)
            return carry

        lax.fori_loop(0, half_blocks, finish_step, 0, unroll=UNROLL)

        copies = []
        for which, (source, target) in enumerate(((key_stage, key_out), (value_stage, value_out))):
            for step in range(half):
                peer = lax.rem(lane + step, half)
                at = devices + which * half + step
                copies.append(transfer(
                    source.at[head, rows(peer, memory_rows), :],
                    target.at[:, columns(lane * heads + head, HEAD_DIM)],
                    step, (group, my_query, side * half + peer),
                    out_send.at[head, at], out_recv.at[head, at], out_own.at[head, which],
                ))
        for copy in copies:
            copy.start()
        returns += copies

    for copy in returns:
        copy.wait()


def head_shards(queries, keys, values, grad_out, blocks):
    memory_size = lax.axis_size("memory")
    devices = lax.axis_size("query") * memory_size
    half = memory_size // 2
    row_count, memory_rows = queries.shape[0], keys.shape[0]
    all_rows, half_rows = row_count * devices, memory_rows * half
    heads = keys.shape[1] // half // HEAD_DIM
    query_blocks, half_blocks = all_rows // BLOCK, half_rows // BLOCK
    slots = 2 * query_blocks
    anywhere = pl.BlockSpec(memory_space=pl.ANY)
    smem = pl.BlockSpec(memory_space=pltpu.SMEM)

    my_query, my_memory = lax.axis_index("query"), lax.axis_index("memory")
    first_head = (my_query * half + my_memory % half) * heads
    picks = lax.dynamic_slice_in_dim(blocks, first_head, heads, 0).reshape(heads, slots)
    picks = picks - my_memory // half * half_blocks
    inside = (picks >= 0) & (picks < half_blocks)
    coded = jnp.where(inside, picks + 1, 0)
    line = jnp.arange(2 * slots + half_blocks, dtype=jnp.int32)[:, None]
    number = jnp.arange(slots, dtype=jnp.int32)[None, :]
    ids = jnp.broadcast_to(jnp.arange(half_blocks, dtype=jnp.int32), (heads, half_blocks))
    wanted = jnp.concatenate([picks, ids, picks], axis=1)[:, :, None]
    first_part = line < slots + half_blocks
    chosen = jnp.where(
        first_part,
        (wanted == picks[:, None, :]) & ((line >= slots) | (number < line)),
        line - slots - half_blocks == number,
    )
    table = jnp.max(
        jnp.where(chosen, jnp.where(first_part, number + 1, coded[:, None, :]), 0), axis=2
    ).reshape(-1)

    def blocked(array):
        return array.reshape(-1, BLOCK, array.shape[1])

    def half_precision(*shape):
        return pltpu.VMEM(shape, jnp.bfloat16)

    def single_precision(*shape):
        return pltpu.VMEM(shape, jnp.float32)

    def semaphores(*shape):
        return pltpu.SemaphoreType.DMA(shape)

    arrivals, returns = 2 * devices + 2 * half, devices + 2 * half
    parts, key_grad, value_grad = pl.pallas_call(
        functools.partial(fused_kernel, devices, half, heads),
        out_shape=(
            jax.ShapeDtypeStruct((2, *queries.shape), jnp.bfloat16),
            jax.ShapeDtypeStruct(keys.shape, jnp.bfloat16),
            jax.ShapeDtypeStruct(values.shape, jnp.bfloat16),
        ),
        in_specs=[smem] + [anywhere] * 4,
        out_specs=(anywhere,) * 3,
        scratch_shapes=[
            half_precision(heads, all_rows, HEAD_DIM),
            half_precision(heads, all_rows, HEAD_DIM),
            [half_precision(half_blocks, BLOCK, HEAD_DIM)] * heads,
            [half_precision(half_blocks, BLOCK, HEAD_DIM)] * heads,
            single_precision(slots, BLOCK, BLOCK),
            single_precision(slots, BLOCK, BLOCK),
            single_precision(heads, 3, query_blocks, BLOCK),
            single_precision(heads, 3, query_blocks, BLOCK),
            single_precision(slots + 1, BLOCK, HEAD_DIM),
            single_precision(slots + 1, BLOCK, HEAD_DIM),
            half_precision(heads, all_rows, HEAD_DIM),
            half_precision(heads, half_rows, HEAD_DIM),
            half_precision(heads, half_rows, HEAD_DIM),
            semaphores(heads, arrivals),
            semaphores(heads, arrivals),
            semaphores(heads, 4),
            semaphores(heads),
            semaphores(heads),
            semaphores(heads, returns),
            semaphores(heads, returns),
            semaphores(heads, 3),
        ],
        compiler_params=pltpu.CompilerParams(
            collective_id=0, has_side_effects=True, vmem_limit_bytes=62 * 1024 * 1024
        ),
        name="head_grads",
    )(table, queries, grad_out, blocked(keys), blocked(values))

    query_grad = parts[0].astype(jnp.float32) + parts[1].astype(jnp.float32)
    return (query_grad.astype(jnp.bfloat16), key_grad, value_grad)


def shards(queries, keys, values, grad_out, blocks):
    memory_size = lax.axis_size("memory")
    whole_heads = keys.shape[1] % (memory_size // 2 * HEAD_DIM) == 0
    if memory_size % 2 == 0 and whole_heads and blocks.shape[2] == 2:
        return head_shards(queries, keys, values, grad_out, blocks)
    return span_shards(queries, keys, values, grad_out, blocks)


def solution(mesh):
    placed = (
        P(("group", "query", "memory"), None),
        P(("group", "memory"), "query"),
        P(("group", "memory"), "query"),
        P(("group", "query", "memory"), None),
        P(None, "group", None),
    )
    return jax.shard_map(
        shards,
        mesh=mesh,
        in_specs=placed,
        out_specs=(
            P(("group", "query", "memory"), None),
            P(("group", "memory"), "query"),
            P(("group", "memory"), "query"),
        ),
        check_vma=False,
    )
```

```python
import functools
import math

import jax
import jax.numpy as jnp
from jax import lax
from jax.experimental import pallas as pl
from jax.experimental.pallas import tpu as pltpu
from jax.sharding import PartitionSpec as P

HEAD_DIM = 128
BLOCK = 128


def joined(value, axis, combine):
    everything = jax.tree.map(lambda part: lax.all_gather(part, axis), value)
    leading = jax.tree.map(lambda part: part[0], everything)

    def hop(k, so_far):
        return combine(so_far, jax.tree.map(lambda part: part[k], everything))

    return lax.fori_loop(1, lax.axis_size(axis), hop, leading)


def combine_stats(first, second):
    top_value = jnp.maximum(first[0], second[0])
    first_factor = jnp.exp(first[0] - top_value)
    second_factor = jnp.exp(second[0] - top_value)
    return (
        top_value,
        first[1] * first_factor + second[1] * second_factor,
        first[2] * first_factor + second[2] * second_factor,
    )


def local_grads(query_rows, grad_rows, key_rows, value_rows, head_blocks, shard_index):
    row_count = query_rows.shape[0]
    query_blocks = row_count // BLOCK
    local_heads = query_rows.shape[1] // HEAD_DIM
    memory_blocks = key_rows.shape[0] // BLOCK
    slot_count = head_blocks.shape[2]
    group_size = math.gcd(query_blocks, 8)
    group_count = query_blocks // group_size
    scale = 1.0 / math.sqrt(HEAD_DIM)

    def split_queries(array):
        return array.reshape(group_count, group_size, BLOCK, local_heads, HEAD_DIM).transpose(
            3, 0, 1, 2, 4
        )

    def split_memory(array):
        return array.reshape(memory_blocks, BLOCK, local_heads, HEAD_DIM).transpose(2, 0, 1, 3)

    query_split = split_queries(query_rows)
    grad_split = split_queries(grad_rows)
    key_split = split_memory(key_rows)
    value_split = split_memory(value_rows)
    local_ids = head_blocks - shard_index * memory_blocks
    live_slots = ((local_ids >= 0) & (local_ids < memory_blocks)).reshape(
        local_heads, group_count, group_size, slot_count
    )
    slot_picks = jnp.clip(local_ids, 0, memory_blocks - 1).reshape(
        local_heads, group_count, group_size, slot_count
    )

    def block_scores(query_group, grad_group, key_head, value_head, picks):
        key_blocks = key_head[picks]
        value_blocks = value_head[picks]
        scores = (
            jnp.einsum(
                "gbd,gskd->gbsk", query_group, key_blocks, preferred_element_type=jnp.float32
            )
            * scale
        )
        prod_grad = jnp.einsum(
            "gbd,gskd->gbsk", grad_group, value_blocks, preferred_element_type=jnp.float32
        )
        return (scores, prod_grad, key_blocks)

    def stats_head(head_inputs):
        query_head, grad_head, key_head, value_head, pick_head, live_head = head_inputs

        def stats_group(group_inputs):
            query_group, grad_group, picks, live_group = group_inputs
            scores, prod_grad, unused_keys = block_scores(
                query_group, grad_group, key_head, value_head, picks
            )
            live_mask = live_group[:, None, :, None]
            top_value = jnp.max(jnp.where(live_mask, scores, -1e30), axis=(2, 3))
            weight = jnp.where(live_mask, jnp.exp(scores - top_value[:, :, None, None]), 0.0)
            return (
                top_value,
                jnp.sum(weight, axis=(2, 3)),
                jnp.sum(weight * prod_grad, axis=(2, 3)),
            )

        return lax.map(stats_group, (query_head, grad_head, pick_head, live_head))

    top_value, total, weighted = lax.map(
        stats_head, (query_split, grad_split, key_split, value_split, slot_picks, live_slots)
    )
    top_value, total, weighted = joined((top_value, total, weighted), "memory", combine_stats)
    log_total = top_value + jnp.log(total)
    delta_row = weighted / total

    def grads_head(head_inputs):
        query_head, grad_head, key_head, value_head, pick_head, live_head, log_head, delta_head = (
            head_inputs
        )

        def grads_group(carry, group_inputs):
            query_group, grad_group, picks, live_group, log_group, delta_group = group_inputs
            scores, prod_grad, key_blocks = block_scores(
                query_group, grad_group, key_head, value_head, picks
            )
            live_mask = live_group[:, None, :, None]
            probs = jnp.where(live_mask, jnp.exp(scores - log_group[:, :, None, None]), 0.0)
            probs_half = probs.astype(jnp.bfloat16)
            score_grad = (probs * (prod_grad - delta_group[:, :, None, None])).astype(jnp.bfloat16)
            value_terms = jnp.einsum(
                "gbsk,gbd->gskd", probs_half, grad_group, preferred_element_type=jnp.float32
            )
            key_terms = (
                jnp.einsum(
                    "gbsk,gbd->gskd", score_grad, query_group, preferred_element_type=jnp.float32
                )
                * scale
            )
            query_terms = (
                jnp.einsum(
                    "gbsk,gskd->gbd", score_grad, key_blocks, preferred_element_type=jnp.float32
                )
                * scale
            )
            flat_picks = picks.reshape(-1)
            flat_live = live_group.reshape(-1)[:, None, None]
            key_total = (
                carry[0]
                .at[flat_picks]
                .add(jnp.where(flat_live, key_terms.reshape(-1, BLOCK, HEAD_DIM), 0.0))
            )
            value_total = (
                carry[1]
                .at[flat_picks]
                .add(jnp.where(flat_live, value_terms.reshape(-1, BLOCK, HEAD_DIM), 0.0))
            )
            return ((key_total, value_total), query_terms)

        zero_grad = jnp.zeros((memory_blocks, BLOCK, HEAD_DIM), jnp.float32)
        totals, query_terms = lax.scan(
            grads_group,
            (zero_grad, zero_grad),
            (query_head, grad_head, pick_head, live_head, log_head, delta_head),
        )
        return (query_terms, totals[0], totals[1])

    query_grad, key_grad, value_grad = lax.map(
        grads_head,
        (
            query_split,
            grad_split,
            key_split,
            value_split,
            slot_picks,
            live_slots,
            log_total,
            delta_row,
        ),
    )
    query_grad = query_grad.transpose(1, 2, 3, 0, 4).reshape(row_count, local_heads * HEAD_DIM)
    key_grad = key_grad.transpose(1, 2, 0, 3).reshape(memory_blocks * BLOCK, local_heads * HEAD_DIM)
    value_grad = value_grad.transpose(1, 2, 0, 3).reshape(
        memory_blocks * BLOCK, local_heads * HEAD_DIM
    )
    return (query_grad, key_grad, value_grad)


def span_shards(queries, keys, values, grad_out, blocks):
    query_span, grad_span = (
        lax.all_gather(queries, "memory", axis=0, tiled=True),
        lax.all_gather(grad_out, "memory", axis=0, tiled=True),
    )
    query_index = lax.axis_index("query")
    memory_index = lax.axis_index("memory")
    key_rows, value_rows = (
        lax.all_gather(keys, "query", axis=1, tiled=True),
        lax.all_gather(values, "query", axis=1, tiled=True),
    )
    span_blocks = query_span.shape[0] // BLOCK
    head_blocks = lax.dynamic_slice_in_dim(blocks, query_index * span_blocks, span_blocks, 1)
    query_part, key_full, value_full = local_grads(
        query_span, grad_span, key_rows, value_rows, head_blocks, memory_index
    )
    key_grad, value_grad = (
        lax.psum_scatter(key_full, "query", scatter_dimension=1, tiled=True),
        lax.psum_scatter(value_full, "query", scatter_dimension=1, tiled=True),
    )
    grad_query = lax.psum_scatter(
        query_part.astype(jnp.bfloat16), "memory", scatter_dimension=0, tiled=True
    )
    return (grad_query, key_grad.astype(jnp.bfloat16), value_grad.astype(jnp.bfloat16))


MESH = pl.DeviceIdType.MESH
NT = (((1,), (1,)), ((), ()))
TN = (((0,), (0,)), ((), ()))
UNROLL = 8


def position():
    memory_size = lax.axis_size("memory")
    here = lax.axis_index("query") * memory_size + lax.axis_index("memory")
    return lax.axis_index("group"), here, memory_size


def meet(group, here, devices, memory_size):
    barrier = pltpu.get_barrier_semaphore()
    for step in range(1, devices):
        peer = lax.rem(here + step, devices)
        pl.semaphore_signal(
            barrier,
            inc=1,
            device_id=(group, peer // memory_size, lax.rem(peer, memory_size)),
            device_id_type=MESH,
        )
    pl.semaphore_wait(barrier, devices - 1)


def columns(index, width):
    return pl.ds(pl.multiple_of(index * width, width), width)


def rows(index, size):
    return pl.ds(pl.multiple_of(index * size, size), size)


def away(group, memory_size, peer):
    return (group, peer // memory_size, lax.rem(peer, memory_size))


def fused_kernel(
    devices, half, heads,
    table, query_ref, grad_ref, key_ref, value_ref,
    parts, key_out, value_out,
    query_in, grad_in, key_in, value_in, weights, products, stats, other, key_sums, value_sums,
    query_stage, key_stage, value_stage,
    in_send, in_recv, in_own, stat_send, stat_recv, out_send, out_recv, out_own,
):
    scale = 1.0 / math.sqrt(HEAD_DIM)
    group, here, memory_size = position()
    my_query, my_memory = here // memory_size, lax.rem(here, memory_size)
    side, lane = my_memory // half, lax.rem(my_memory, half)
    partner = (group, my_query, lax.rem(my_memory + half, memory_size))
    row_count, own_blocks = query_ref.shape[0], key_ref.shape[0]
    memory_rows = own_blocks * BLOCK
    query_blocks = query_in.shape[1] // BLOCK
    half_blocks = key_in[0].shape[0]
    slots = 2 * query_blocks
    lines = 2 * slots + half_blocks
    meet(group, here, devices, memory_size)

    query_size = devices // memory_size
    peers = []
    for hop in (*range(memory_size // 2, 0, -1), *range(memory_size // 2 + 1, memory_size), 0):
        for turn in range(query_size):
            peer_query = lax.rem(my_query + turn, query_size)
            peer_memory = lax.rem(my_memory + hop, memory_size)
            peers.append((hop * query_size + turn, peer_query * memory_size + peer_memory))

    def transfer(source, target, step, device, send, recv, own):
        if step == 0:
            return pltpu.make_async_copy(source, target, own)
        return pltpu.make_async_remote_copy(
            src_ref=source, dst_ref=target, send_sem=send, recv_sem=recv,
            device_id=device, device_id_type=MESH,
        )

    arrivals = []
    for head in range(heads):
        copies = []
        for which, (source, target) in enumerate(((key_ref, key_in), (value_ref, value_in))):
            for step in range(half):
                peer = lax.rem(lane + step, half)
                at = 2 * devices + which * half + step
                copies.append(transfer(
                    source.at[:, :, columns(peer * heads + head, HEAD_DIM)],
                    target[head].at[pl.ds(lane * own_blocks, own_blocks)],
                    step, (group, my_query, side * half + peer),
                    in_send.at[head, at], in_recv.at[head, at], in_own.at[head, which],
                ))
        for step, peer in peers:
            first = (peer // memory_size * half + lax.rem(lax.rem(peer, memory_size), half)) * heads
            for which, (source, target) in enumerate(((query_ref, query_in), (grad_ref, grad_in))):
                at = which * devices + step
                copies.append(transfer(
                    source.at[:, columns(first + head, HEAD_DIM)],
                    target.at[head, rows(here, row_count), :],
                    step, away(group, memory_size, peer),
                    in_send.at[head, at], in_recv.at[head, at], in_own.at[head, 2 + which],
                ))
        for copy in copies:
            copy.start()
        arrivals.append(copies)

    key_sums[0] = jnp.zeros(key_sums.shape[1:], jnp.float32)
    value_sums[0] = jnp.zeros(value_sums.shape[1:], jnp.float32)
    returns = []
    for head in range(heads):
        for copy in arrivals[head]:
            copy.wait()

        def pick(block, slot):
            coded = table[head * lines + slots + half_blocks + 2 * block + slot]
            return jnp.maximum(coded - 1, 0), jnp.minimum(coded, 1).astype(jnp.float32)

        def stats_step(block, carry):
            mine = rows(block, BLOCK)
            query, grad = query_in[head, mine, :], grad_in[head, mine, :]
            scores = []
            for slot in range(2):
                place, live = pick(block, slot)
                score = lax.dot_general(
                    key_in[head][place], query, NT, preferred_element_type=jnp.float32
                )
                scores.append(score * (scale * live) + (live - 1.0) * 1e30)
                products[2 * block + slot] = lax.dot_general(
                    value_in[head][place], grad, NT, preferred_element_type=jnp.float32
                )
            top = jnp.maximum(
                jnp.max(scores[0], axis=0, keepdims=True), jnp.max(scores[1], axis=0, keepdims=True)
            )
            total, weighted = 0.0, 0.0
            for slot in range(2):
                place, live = pick(block, slot)
                weight = jnp.exp(scores[slot] - top) * live
                weights[2 * block + slot] = weight
                total += jnp.sum(weight, axis=0, keepdims=True)
                weighted += jnp.sum(weight * products[2 * block + slot], axis=0, keepdims=True)
            line = pl.ds(block, 1)
            stats[head, 0, line, :] = top
            stats[head, 1, line, :] = total
            stats[head, 2, line, :] = weighted
            return carry

        lax.fori_loop(0, query_blocks, stats_step, 0, unroll=UNROLL)
        exchange = pltpu.make_async_remote_copy(
            src_ref=stats.at[head], dst_ref=other.at[head],
            send_sem=stat_send.at[head], recv_sem=stat_recv.at[head],
            device_id=partner, device_id_type=MESH,
        )
        exchange.start()
        exchange.wait()
        ours = (stats[head, 0], stats[head, 1], stats[head, 2])
        top, total, weighted = combine_stats(ours, (other[head, 0], other[head, 1], other[head, 2]))
        stats[head, 0] = jnp.exp(ours[0] - top) / total
        stats[head, 1] = weighted / total

        def grads_step(block, carry):
            mine, line = rows(block, BLOCK), pl.ds(block, 1)
            query, grad = query_in[head, mine, :], grad_in[head, mine, :]
            factor, delta = stats[head, 0, line, :], stats[head, 1, line, :]
            query_term = 0.0
            plain = (((1,), (0,)), ((), ()))
            key_terms, value_terms = [], []
            for slot in range(2):
                place, live = pick(block, slot)
                number = 2 * block + slot
                probs = weights[number] * factor
                score_grad = (probs * (products[number] - delta)).astype(jnp.bfloat16)
                value_terms.append(lax.dot_general(
                    probs.astype(jnp.bfloat16), grad, plain, preferred_element_type=jnp.float32
                ))
                key_terms.append(lax.dot_general(
                    score_grad, query, plain, preferred_element_type=jnp.float32
                ))
                query_term += lax.dot_general(
                    score_grad, key_in[head][place], TN, preferred_element_type=jnp.float32
                )
            query_stage[head, mine, :] = (query_term * scale).astype(query_stage.dtype)
            for slot in range(2):
                number = 2 * block + slot
                before = table[head * lines + number]
                key_sums[number + 1] = key_sums[before] + key_terms[slot]
                value_sums[number + 1] = value_sums[before] + value_terms[slot]
            return carry

        lax.fori_loop(0, query_blocks, grads_step, 0, unroll=UNROLL)

        copies = []
        for step, peer in peers:
            copies.append(transfer(
                query_stage.at[head, rows(peer, row_count), :],
                parts.at[side, :, columns((my_query * half + lane) * heads + head, HEAD_DIM)],
                step, away(group, memory_size, peer),
                out_send.at[head, step], out_recv.at[head, step], out_own.at[head, 2],
            ))
        for copy in copies:
            copy.start()
        returns += copies

        def finish_step(block, carry):
            last = table[head * lines + slots + block]
            mine = rows(block, BLOCK)
            key_stage[head, mine, :] = (key_sums[last] * scale).astype(key_stage.dtype)
            value_stage[head, mine, :] = value_sums[last].astype(value_stage.dtype)
            return carry

        lax.fori_loop(0, half_blocks, finish_step, 0, unroll=UNROLL)

        copies = []
        for which, (source, target) in enumerate(((key_stage, key_out), (value_stage, value_out))):
            for step in range(half):
                peer = lax.rem(lane + step, half)
                at = devices + which * half + step
                copies.append(transfer(
                    source.at[head, rows(peer, memory_rows), :],
                    target.at[:, columns(lane * heads + head, HEAD_DIM)],
                    step, (group, my_query, side * half + peer),
                    out_send.at[head, at], out_recv.at[head, at], out_own.at[head, which],
                ))
        for copy in copies:
            copy.start()
        returns += copies

    for copy in returns:
        copy.wait()


def head_shards(queries, keys, values, grad_out, blocks):
    memory_size = lax.axis_size("memory")
    devices = lax.axis_size("query") * memory_size
    half = memory_size // 2
    row_count, memory_rows = queries.shape[0], keys.shape[0]
    all_rows, half_rows = row_count * devices, memory_rows * half
    heads = keys.shape[1] // half // HEAD_DIM
    query_blocks, half_blocks = all_rows // BLOCK, half_rows // BLOCK
    slots = 2 * query_blocks
    anywhere = pl.BlockSpec(memory_space=pl.ANY)
    smem = pl.BlockSpec(memory_space=pltpu.SMEM)

    my_query, my_memory = lax.axis_index("query"), lax.axis_index("memory")
    first_head = (my_query * half + my_memory % half) * heads
    picks = lax.dynamic_slice_in_dim(blocks, first_head, heads, 0).reshape(heads, slots)
    picks = picks - my_memory // half * half_blocks
    inside = (picks >= 0) & (picks < half_blocks)
    coded = jnp.where(inside, picks + 1, 0)
    line = jnp.arange(2 * slots + half_blocks, dtype=jnp.int32)[:, None]
    number = jnp.arange(slots, dtype=jnp.int32)[None, :]
    ids = jnp.broadcast_to(jnp.arange(half_blocks, dtype=jnp.int32), (heads, half_blocks))
    wanted = jnp.concatenate([picks, ids, picks], axis=1)[:, :, None]
    first_part = line < slots + half_blocks
    chosen = jnp.where(
        first_part,
        (wanted == picks[:, None, :]) & ((line >= slots) | (number < line)),
        line - slots - half_blocks == number,
    )
    table = jnp.max(
        jnp.where(chosen, jnp.where(first_part, number + 1, coded[:, None, :]), 0), axis=2
    ).reshape(-1)

    def blocked(array):
        return array.reshape(-1, BLOCK, array.shape[1])

    def half_precision(*shape):
        return pltpu.VMEM(shape, jnp.bfloat16)

    def single_precision(*shape):
        return pltpu.VMEM(shape, jnp.float32)

    def semaphores(*shape):
        return pltpu.SemaphoreType.DMA(shape)

    arrivals, returns = 2 * devices + 2 * half, devices + 2 * half
    parts, key_grad, value_grad = pl.pallas_call(
        functools.partial(fused_kernel, devices, half, heads),
        out_shape=(
            jax.ShapeDtypeStruct((2, *queries.shape), jnp.bfloat16),
            jax.ShapeDtypeStruct(keys.shape, jnp.bfloat16),
            jax.ShapeDtypeStruct(values.shape, jnp.bfloat16),
        ),
        in_specs=[smem] + [anywhere] * 4,
        out_specs=(anywhere,) * 3,
        scratch_shapes=[
            half_precision(heads, all_rows, HEAD_DIM),
            half_precision(heads, all_rows, HEAD_DIM),
            [half_precision(half_blocks, BLOCK, HEAD_DIM)] * heads,
            [half_precision(half_blocks, BLOCK, HEAD_DIM)] * heads,
            single_precision(slots, BLOCK, BLOCK),
            single_precision(slots, BLOCK, BLOCK),
            single_precision(heads, 3, query_blocks, BLOCK),
            single_precision(heads, 3, query_blocks, BLOCK),
            single_precision(slots + 1, BLOCK, HEAD_DIM),
            single_precision(slots + 1, BLOCK, HEAD_DIM),
            half_precision(heads, all_rows, HEAD_DIM),
            half_precision(heads, half_rows, HEAD_DIM),
            half_precision(heads, half_rows, HEAD_DIM),
            semaphores(heads, arrivals),
            semaphores(heads, arrivals),
            semaphores(heads, 4),
            semaphores(heads),
            semaphores(heads),
            semaphores(heads, returns),
            semaphores(heads, returns),
            semaphores(heads, 3),
        ],
        compiler_params=pltpu.CompilerParams(
            collective_id=0, has_side_effects=True, vmem_limit_bytes=62 * 1024 * 1024
        ),
        name="head_grads",
    )(table, queries, grad_out, blocked(keys), blocked(values))

    query_grad = parts[0].astype(jnp.float32) + parts[1].astype(jnp.float32)
    return (query_grad.astype(jnp.bfloat16), key_grad, value_grad)


def shards(queries, keys, values, grad_out, blocks):
    memory_size = lax.axis_size("memory")
    whole_heads = keys.shape[1] % (memory_size // 2 * HEAD_DIM) == 0
    if memory_size % 2 == 0 and whole_heads and blocks.shape[2] == 2:
        return head_shards(queries, keys, values, grad_out, blocks)
    return span_shards(queries, keys, values, grad_out, blocks)


def solution(mesh):
    placed = (
        P(("group", "query", "memory"), None),
        P(("group", "memory"), "query"),
        P(("group", "memory"), "query"),
        P(("group", "query", "memory"), None),
        P(None, "group", None),
    )
    return jax.shard_map(
        shards,
        mesh=mesh,
        in_specs=placed,
        out_specs=(
            P(("group", "query", "memory"), None),
            P(("group", "memory"), "query"),
            P(("group", "memory"), "query"),
        ),
        check_vma=False,
    )
```
